256 devices in a mesh: region: 16 (over x, y), shard: 16 (over z, core).
Axes of the slice: x: 4, y: 4, z: 8, core: 2. Of those that a mesh axis runs over, the one named last changes fastest.
Arguments:
- query_feats: bfloat16 [65536, 512], P(('region', 'shard')), may hold values from -6 to 6
- query_region: int32 [65536, 1], P(('region', 'shard')), may hold values from 0 to 15; in each aligned block of 256 rows (0 to 255, 256 to 511, ...) at most 32 rows name the same one
- neighbors: int32 [65536, 64], P(('region', 'shard')), may hold values from 0 to 1023
- latents: bfloat16 [16384, 512], P(('region', 'shard')), may hold values from -380 to 380
- w_query: bfloat16 [512, 512], replicated, may hold values from -0.25 to 0.25
- w_key: bfloat16 [512, 512], replicated, may hold values from -0.25 to 0.25
- w_value: bfloat16 [512, 512], replicated, may hold values from -0.25 to 0.25
- w_out: bfloat16 [512, 512], replicated, may hold values from -0.25 to 0.25
- norm_gain: float32 [512], replicated, may hold values from 0.1 to 1.9
- w_up: bfloat16 [512, 2048], replicated, may hold values from -0.25 to 0.25
- w_down: bfloat16 [2048, 512], replicated, may hold values from -0.125 to 0.125
Outputs:
- refined: bfloat16 [65536, 512], P(('region', 'shard'))
The draws below stay inside these ranges and needn't reach their ends.
Inputs may be any that keep to these rules, and one draw needn't show every extreme that they name: `query_region`: among the queries of one device (aligned blocks of 256 rows) no region is named more than 32 times, a bound that some block reaches.
All inputs are finite; a program needn't handle non-finite values.
Results may differ from the reference program's by a relative error of at most 0.012.
The reference program's roundings to bfloat16 on the way (of `query_proj`, `weights`, `mixed`, `normed` and `hidden`) count: a program that leaves them out, or rounds other values in their place, can miss the bound.
Values may be sent and summed in bfloat16 or wider, within the bound.
No kernel may reach another device: no remote copies, remote signals or barrier semaphores. Data moves between devices by JAX's collectives and lax.ppermute only.
A program may use at most 64 MiB of HBM per device.

```python
import math
import jax
import jax.numpy as jnp
import numpy as np
from jax import lax

D = 512
FF = 2048
HEADS = 4
HEAD_DIM = 128
KNB = 64
Q_DEV = 256
CAP = 32
L_REG = 1024
LATENTS = 16384
QUERIES = 65536
N_REGION = 16


def draw_latents(key, part):
    base = jax.random.normal(jax.random.fold_in(key, 11), (LATENTS, D), jnp.float32)
    return jnp.clip(base, -6.0, 6.0).astype(jnp.bfloat16)


def set_ends(array, key, least, high):
    index_at = [jax.random.randint(jax.random.fold_in(key, axis), (), 0, length) for axis, length in enumerate(array.shape)]
    widest = array.shape.index(max(array.shape))
    neighbour = index_at[:widest] + [(index_at[widest] + 1) % array.shape[widest]] + index_at[widest + 1:]
    return array.at[tuple(index_at)].set(least).at[tuple(neighbour)].set(high)


def steps_of(stream_key, shape, shards, smallest, high):
    def one(position, parts):
        heights = jax.random.uniform(jax.random.fold_in(jax.random.fold_in(stream_key, 6), position), (parts,), jnp.float32, smallest / len(shards), high / len(shards))
        return jnp.repeat(jnp.exp(heights), shape[position] // parts).reshape((-1,) + (1,) * (len(shape) - position - 1))

    gain = one(*shards[0])
    for cut in shards[1:]:
        gain = gain * one(*cut)
    return gain


def shared_out(rng, own, number, rows, number_of, top, bound, slope):
    order = jax.random.permutation(rng, number_of)
    heavy_load, common = portions_of(number_of, rows * top, bound, slope, True), portions_of(number_of, rows * top, bound, slope, False)
    places = jnp.arange(number_of)

    def named(sizes, turn):
        used = int((sizes > 0).sum())
        fixed = max(1, used // 4)
        moved = fixed + (places - fixed + turn * (used - fixed)) % max(1, number_of - fixed)
        return jnp.zeros((number_of,), jnp.int32).at[order[jnp.where(places < fixed, places, moved)]].set(jnp.asarray(sizes, jnp.int32))

    sizes = jnp.where(number % 4 == 0, named(heavy_load, number // 4), named(common, number - number // 4 - 1))
    mixed = jax.random.permutation(jax.random.fold_in(own, 3), number_of)
    giver, receiver = mixed[0:number_of // 2 * 2:2], mixed[1:number_of // 2 * 2:2]
    room = jnp.minimum(sizes[giver] - 1, bound - sizes[receiver]) // 2
    room = jnp.where((giver == order[0]) | (receiver == order[0]) | (sizes[receiver] == 0), 0, jnp.maximum(room, 0))
    moved = jax.random.randint(jax.random.fold_in(own, 4), (number_of // 2,), 0, 1 << 20) % (room + 1)
    sizes = sizes.at[giver].add(-moved).at[receiver].add(moved)
    members = jnp.searchsorted(jnp.cumsum(sizes), jnp.arange(rows * top), side="right").astype(jnp.int32)
    table = members.reshape(top, rows).T
    table = table[jax.random.permutation(jax.random.fold_in(own, 1), rows)]
    turn = jax.random.randint(jax.random.fold_in(own, 2), (rows, 1), 0, top)
    return jnp.take_along_axis(table, (jnp.arange(top)[None, :] + turn) % top, axis=1)


def portions_of(number_of, total, most, slope, full):
    weights = [(1 << 20) // math.isqrt(standing ** slope) + 1 for standing in range(1, number_of + 1)]
    largest = most if full else min(most, max(-(-total // number_of), total * weights[0] // sum(weights)))
    least = 1 if total - largest >= number_of - 1 else 0
    counts, surplus = [largest] + [least] * (number_of - 1), total - largest - least * (number_of - 1)
    while surplus > 0:
        movable = [i for i in range(1, number_of) if counts[i] < largest] or [i for i in range(1, number_of) if counts[i] < most]
        whole, remaining = sum([weights[i] for i in movable]), surplus
        for i in movable:
            more = min(most - counts[i], max(1, remaining * weights[i] // whole), surplus)
            counts[i] = counts[i] + more
            surplus = surplus - more
    return np.array(counts)


def scatter_about(rng, extent, scale, bound, split=(), kind=jnp.bfloat16):
    level = steps_of(rng, extent, split, -0.22, 0.18) if split else 1.0
    entries = jax.random.normal(rng, extent, jnp.float32) * scale * level
    return jnp.minimum(jnp.maximum(entries, -bound), bound).astype(kind)


def setup_inputs(seed: int = 0) -> dict:
    key_of = jax.random.split(jax.random.key(seed), 12)
    query_feats = scatter_about(key_of[0], (QUERIES, D), 1.0, 6.0, ((0, 256),))
    query_region_keys = jax.random.split(jax.random.fold_in(key_of[1], 1), QUERIES // Q_DEV)
    query_region_turns = jax.random.permutation(jax.random.fold_in(key_of[1], 3), QUERIES // Q_DEV)
    query_region = jax.vmap(lambda own, number: shared_out(jax.random.fold_in(key_of[1], 2), own, number, Q_DEV, N_REGION, 1, CAP, 2))(query_region_keys, query_region_turns).reshape((QUERIES, 1))
    neighbors = set_ends(jax.random.randint(key_of[2], (QUERIES, KNB), 0, L_REG), jax.random.fold_in(key_of[2], 1), 0, L_REG - 1).astype(jnp.int32)
    latents = draw_latents(jax.random.fold_in(key_of[11], 71), 0)
    w_query = scatter_about(key_of[4], (D, D), D ** -0.5, 0.25)
    w_key = scatter_about(key_of[5], (D, D), D ** -0.5, 0.25)
    w_value = scatter_about(key_of[6], (D, D), D ** -0.5, 0.25)
    w_out = scatter_about(key_of[7], (D, D), D ** -0.5, 0.25)
    norm_gain = jnp.clip(1.0 + 0.18 * jax.random.normal(key_of[8], (D,), jnp.float32), 0.1, 1.9)
    w_up = scatter_about(key_of[9], (D, FF), D ** -0.5, 0.25)
    w_down = scatter_about(key_of[10], (FF, D), FF ** -0.5, 0.125)
    return dict(query_feats=query_feats, query_region=query_region, neighbors=neighbors, latents=latents, w_query=w_query, w_key=w_key, w_value=w_value, w_out=w_out, norm_gain=norm_gain, w_up=w_up, w_down=w_down)


def refine_rows(features, row_index, key_table, value_table, w_query, w_out, norm_gain, w_up, w_down):
    slot_count = features.shape[0]
    neighbor_count = row_index.shape[1]
    query_proj = jnp.dot(features, w_query, preferred_element_type=jnp.float32).astype(jnp.bfloat16)
    key_rows = jnp.take(key_table, row_index, axis=0).reshape(slot_count, neighbor_count, HEADS, HEAD_DIM)
    scores = jnp.einsum('shd,skhd->shk', query_proj.reshape(slot_count, HEADS, HEAD_DIM).astype(jnp.float32), key_rows.astype(jnp.float32)) * HEAD_DIM ** (-0.5)
    peak = lax.optimization_barrier(jnp.max(scores, axis=2, keepdims=True))
    raised = jnp.exp(scores - peak)
    weights = (raised / lax.optimization_barrier(jnp.sum(raised, axis=2, keepdims=True))).astype(jnp.bfloat16)
    value_rows = jnp.take(value_table, row_index, axis=0).reshape(slot_count, neighbor_count, HEADS, HEAD_DIM)
    mixed = jnp.einsum('shk,skhd->shd', weights.astype(jnp.float32), value_rows.astype(jnp.float32))
    mixed = mixed.reshape(slot_count, HEADS * HEAD_DIM).astype(jnp.bfloat16)
    resid = features.astype(jnp.float32) + jnp.dot(mixed, w_out, preferred_element_type=jnp.float32)
    meansq = lax.optimization_barrier(jnp.mean(resid * resid, axis=1, keepdims=True))
    normed = (resid * lax.rsqrt(meansq + 1e-05) * norm_gain).astype(jnp.bfloat16)
    hidden = jax.nn.gelu(jnp.dot(normed, w_up, preferred_element_type=jnp.float32), approximate=True).astype(jnp.bfloat16)
    return (resid + jnp.dot(hidden, w_down, preferred_element_type=jnp.float32)).astype(jnp.bfloat16)

def reference(query_feats, query_region, neighbors, latents, w_query, w_key, w_value, w_out, norm_gain, w_up, w_down):
    key_table = jnp.dot(latents, w_key, preferred_element_type=jnp.float32).astype(jnp.bfloat16)
    value_table = jnp.dot(latents, w_value, preferred_element_type=jnp.float32).astype(jnp.bfloat16)
    row_index = (query_region[:, :1].astype(jnp.int32) * L_REG + neighbors.astype(jnp.int32)).astype(jnp.int32)
    block_count = QUERIES // Q_DEV
    feature_blocks = query_feats.reshape(block_count, Q_DEV, D)
    index_blocks = row_index.reshape(block_count, Q_DEV, KNB)

    def one_block(pair):
        return refine_rows(pair[0], pair[1], key_table, value_table, w_query, w_out, norm_gain, w_up, w_down)
    refined = lax.map(one_block, (feature_blocks, index_blocks))
    return refined.reshape(QUERIES, D)
```

```python
import functools
import math

import jax
import jax.numpy as jnp
from jax import lax
from jax.experimental import pallas as pl
from jax.experimental.pallas import tpu as pltpu
from jax.sharding import PartitionSpec as P

HEADS = 4
LANES = 128
ABSENT = -1e30
F32 = jnp.float32
BF16 = jnp.bfloat16
VMEM = pl.BlockSpec(memory_space=pltpu.VMEM)
NT = (((1,), (1,)), ((), ()))


def slots_of(region_row, region_count, capacity):
    rows = region_row.shape[1]
    onehot = (lax.broadcasted_iota(jnp.int32, (region_count, rows), 0) == region_row).astype(F32)
    earlier_than = lax.broadcasted_iota(jnp.int32, (rows, rows), 0) < lax.broadcasted_iota(
        jnp.int32, (rows, rows), 1
    )
    earlier = jnp.dot(onehot.astype(BF16), earlier_than.astype(BF16), preferred_element_type=F32)
    rank = jnp.sum(earlier * onehot, axis=0, keepdims=True)
    return region_row.astype(F32) * float(capacity) + rank


def pack_kernel(region_count, capacity, feats_ref, region_ref, neighbors_ref, w_query_ref, send_ref):
    slot_count = region_count * capacity
    rows, width = feats_ref.shape
    neighbor_count = neighbors_ref.shape[0]
    slot_row = slots_of(region_ref[...], region_count, capacity)
    place = (
        lax.broadcasted_iota(jnp.int32, (slot_count, rows), 0).astype(F32) == slot_row
    ).astype(BF16)
    query = jnp.dot(feats_ref[...], w_query_ref[...], preferred_element_type=F32).astype(BF16)
    send_ref[:, :width] = jnp.dot(place, query, preferred_element_type=F32).astype(BF16)
    number = neighbors_ref[...]
    coded = ((number & 127) + 128) << (number >> 7)
    coded = coded.astype(F32).astype(BF16)
    spread = lax.dot_general(place, coded, NT, preferred_element_type=F32).astype(BF16)
    filler = jnp.zeros((slot_count, send_ref.shape[1] - width - neighbor_count), BF16)
    send_ref[:, width:] = jnp.concatenate([spread, filler], axis=1)


def count_kernel(neighbor_count, received_ref, logcount_ref, low_ref, digit_ref):
    slot_count = logcount_ref.shape[1]
    coded = received_ref[...].astype(F32)
    for block in range(slot_count // LANES):
        part = jnp.transpose(coded[block * LANES : (block + 1) * LANES])[:neighbor_count]
        high = jnp.zeros(part.shape, jnp.int32)
        for power in range(1, 8):
            high += (part >= float(128 << power)).astype(jnp.int32)
        value = part.astype(jnp.int32)
        low_ref[block] = (value >> high) - 128
        digit_ref[block] = jnp.int32(1) << (4 * high)

    def one(step, carry):
        block, half = step // 2, step % 2
        base = half * 64
        lanes = pl.ds(pl.multiple_of(block * LANES, LANES), LANES)
        rows = lax.broadcasted_iota(jnp.int32, (64, LANES), 0) + base
        even = jnp.zeros((64, LANES), jnp.int32)
        odd = jnp.zeros((64, LANES), jnp.int32)
        for first in range(0, neighbor_count, 13):
            total = jnp.zeros((64, LANES), jnp.int32)
            for k in range(first, min(first + 13, neighbor_count)):
                same = low_ref[block, k : k + 1, :] == rows
                total = total + jnp.where(same, digit_ref[block, k : k + 1, :], 0)
            even = even + (total & 0x0F0F0F0F)
            odd = odd + ((total >> 4) & 0x0F0F0F0F)
        for high in range(8):
            field = ((odd if high % 2 else even) >> (8 * (high // 2))) & 0xFF
            logs = jnp.where(field > 0, jnp.log2(field.astype(F32)), ABSENT)
            target = pl.ds(pl.multiple_of(high * LANES + base, 64), 64)
            logcount_ref[target, lanes] = logs
        return carry

    lax.fori_loop(0, slot_count // LANES * 2, one, 0)


def attend_kernel(
    query_ref, logcount_ref, near_ref, far_ref, w_key_ref, w_value_ref, mixed_ref, token_ref, key_ref, value_ref
):
    slot_count, width = query_ref.shape
    head_width = width // HEADS
    half_rows = near_ref.shape[0]
    chips = half_rows // 64
    place = lax.axis_index("shard")
    chip, core = place // 2, place % 2
    for step in range(chips):
        origin = lax.rem(chip - step + chips, chips) * 2
        piece = slice(step * 64, step * 64 + 64)
        token_ref[pl.ds(pl.multiple_of((origin + core) * 64, 64), 64), :] = near_ref[piece, :]
        token_ref[pl.ds(pl.multiple_of((origin + 1 - core) * 64, 64), 64), :] = far_ref[piece, :]
    tokens = token_ref[...]
    key_ref[...] = jnp.dot(tokens, w_key_ref[...], preferred_element_type=F32).astype(BF16)
    value_ref[...] = lax.dot_general(
        w_value_ref[...], tokens, (((0,), (1,)), ((), ())), preferred_element_type=F32
    ).astype(BF16)
    factor = head_width ** (-0.5) * math.log2(math.e)
    size = 256
    for block in range(slot_count // size):
        rows = slice(block * size, (block + 1) * size)
        for head in range(HEADS):
            columns = slice(head * head_width, (head + 1) * head_width)
            scores = lax.dot_general(
                key_ref[:, columns], query_ref[rows, columns], NT, preferred_element_type=F32
            )
            scores = scores * factor + logcount_ref[:, rows]
            peak = jnp.max(scores, axis=0, keepdims=True)
            raised = jnp.exp2(scores - peak)
            total = jnp.sum(raised, axis=0, keepdims=True)
            mixed = jnp.dot(value_ref[columns, :], raised.astype(BF16), preferred_element_type=F32)
            mixed_ref[rows, columns] = jnp.transpose(mixed / total).astype(BF16)


def finish_kernel(
    region_count,
    capacity,
    feats_ref,
    region_ref,
    returned_ref,
    w_out_ref,
    gain_ref,
    w_up_ref,
    w_down_ref,
    refined_ref,
):
    rows = feats_ref.shape[0]
    slot_count = region_count * capacity
    slot_row = slots_of(region_ref[...], region_count, capacity)
    slot_column = jnp.transpose(jnp.broadcast_to(slot_row, (LANES, rows)))
    pick = jnp.concatenate(
        [
            (lax.broadcasted_iota(jnp.int32, (rows, LANES), 1) + first).astype(F32) == slot_column
            for first in range(0, slot_count, LANES)
        ],
        axis=1,
    ).astype(BF16)
    mixed = jnp.dot(pick, returned_ref[...], preferred_element_type=F32).astype(BF16)
    resid = feats_ref[...].astype(F32) + jnp.dot(
        mixed, w_out_ref[...], preferred_element_type=F32
    )
    meansq = jnp.mean(resid * resid, axis=1, keepdims=True)
    normed = (resid * lax.rsqrt(meansq + 1e-05) * gain_ref[...]).astype(BF16)
    hidden = jax.nn.gelu(
        jnp.dot(normed, w_up_ref[...], preferred_element_type=F32), approximate=True
    ).astype(BF16)
    refined_ref[...] = (
        resid + jnp.dot(hidden, w_down_ref[...], preferred_element_type=F32)
    ).astype(BF16)


def params(mebibytes):
    return pltpu.CompilerParams(vmem_limit_bytes=mebibytes << 20)


def on_device(
    query_feats,
    query_region,
    neighbors,
    latents,
    w_query,
    w_key,
    w_value,
    w_out,
    norm_gain,
    w_up,
    w_down,
):
    region_count = lax.axis_size("region")
    shard_count = lax.axis_size("shard")
    chips = shard_count // 2
    query_count, width = query_feats.shape
    neighbor_count = neighbors.shape[1]
    capacity = min(query_count, 2 * query_count // region_count)
    slot_count = region_count * capacity
    wide = width + LANES
    table_rows = latents.shape[0] * shard_count
    region_row = query_region.reshape(1, query_count)

    def ring(step):
        return [
            (chip * 2 + core, (chip + step) % chips * 2 + core)
            for chip in range(chips)
            for core in range(2)
        ]

    pieces = [latents] + [lax.ppermute(latents, "shard", ring(step)) for step in range(1, chips)]
    send = pl.pallas_call(
        functools.partial(pack_kernel, region_count, capacity),
        out_shape=jax.ShapeDtypeStruct((slot_count, wide), BF16),
        in_specs=[VMEM] * 4,
        out_specs=VMEM,
        compiler_params=params(12),
        name="pack",
    )(query_feats, region_row, neighbors.T, w_query)
    received = lax.all_to_all(
        send.reshape(region_count, capacity, wide), "region", split_axis=0, concat_axis=0, tiled=True
    ).reshape(slot_count, wide)
    near = jnp.concatenate(pieces, axis=0)
    far = lax.ppermute(
        near, "shard", [(place, place + 1 - 2 * (place % 2)) for place in range(shard_count)]
    )
    logcount = pl.pallas_call(
        functools.partial(count_kernel, neighbor_count),
        grid=(1,),
        out_shape=jax.ShapeDtypeStruct((table_rows, slot_count), F32),
        in_specs=[pl.BlockSpec((slot_count, LANES), lambda i: (0, width // LANES))],
        out_specs=pl.BlockSpec((table_rows, slot_count), lambda i: (0, 0)),
        scratch_shapes=[
            pltpu.VMEM((slot_count // LANES, neighbor_count, LANES), jnp.int32),
            pltpu.VMEM((slot_count // LANES, neighbor_count, LANES), jnp.int32),
        ],
        compiler_params=params(12),
        name="count",
    )(received)
    mixed = pl.pallas_call(
        attend_kernel,
        grid=(1,),
        out_shape=jax.ShapeDtypeStruct((slot_count, width), BF16),
        in_specs=[
            pl.BlockSpec((slot_count, width), lambda i: (0, 0)),
            pl.BlockSpec((table_rows, slot_count), lambda i: (0, 0)),
            pl.BlockSpec(near.shape, lambda i: (0, 0)),
            pl.BlockSpec(near.shape, lambda i: (0, 0)),
            pl.BlockSpec(w_key.shape, lambda i: (0, 0)),
            pl.BlockSpec(w_value.shape, lambda i: (0, 0)),
        ],
        out_specs=pl.BlockSpec((slot_count, width), lambda i: (0, 0)),
        scratch_shapes=[
            pltpu.VMEM((table_rows, width), BF16),
            pltpu.VMEM((table_rows, width), BF16),
            pltpu.VMEM((width, table_rows), BF16),
        ],
        compiler_params=params(32),
        name="attend",
    )(received, logcount, near, far, w_key, w_value)
    returned = lax.all_to_all(
        mixed.reshape(region_count, capacity, width), "region", split_axis=0, concat_axis=0, tiled=True
    ).reshape(slot_count, width)
    return pl.pallas_call(
        functools.partial(finish_kernel, region_count, capacity),
        out_shape=jax.ShapeDtypeStruct((query_count, width), BF16),
        in_specs=[VMEM] * 7,
        out_specs=VMEM,
        compiler_params=params(24),
        name="finish",
    )(query_feats, region_row, returned, w_out, norm_gain.reshape(1, width), w_up, w_down)


def solution(mesh):
    in_specs = (P(("region", "shard"), None),) * 4 + (P(),) * 7
    out_specs = P(("region", "shard"), None)
    return jax.shard_map(
        on_device, mesh=mesh, in_specs=in_specs, out_specs=out_specs, check_vma=False
    )
```

```python
import functools
import math

import jax
import jax.numpy as jnp
from jax import lax
from jax.experimental import pallas as pl
from jax.experimental.pallas import tpu as pltpu
from jax.sharding import PartitionSpec as P

HEADS = 4
LANES = 128
ABSENT = -1e30
F32 = jnp.float32
BF16 = jnp.bfloat16
VMEM = pl.BlockSpec(memory_space=pltpu.VMEM)
NT = (((1,), (1,)), ((), ()))


def slots_of(region_row, region_count, capacity):
    rows = region_row.shape[1]
    onehot = (lax.broadcasted_iota(jnp.int32, (region_count, rows), 0) == region_row).astype(F32)
    earlier_than = lax.broadcasted_iota(jnp.int32, (rows, rows), 0) < lax.broadcasted_iota(
        jnp.int32, (rows, rows), 1
    )
    earlier = jnp.dot(onehot.astype(BF16), earlier_than.astype(BF16), preferred_element_type=F32)
    rank = jnp.sum(earlier * onehot, axis=0, keepdims=True)
    return region_row.astype(F32) * float(capacity) + rank


def pack_kernel(region_count, capacity, feats_ref, region_ref, neighbors_ref, w_query_ref, latents_ref, send_ref, held_ref):
    held_ref[...] = latents_ref[...]
    slot_count = region_count * capacity
    rows, width = feats_ref.shape
    neighbor_count = neighbors_ref.shape[0]
    slot_row = slots_of(region_ref[...], region_count, capacity)
    place = (
        lax.broadcasted_iota(jnp.int32, (slot_count, rows), 0).astype(F32) == slot_row
    ).astype(BF16)
    query = jnp.dot(feats_ref[...], w_query_ref[...], preferred_element_type=F32).astype(BF16)
    send_ref[:, :width] = jnp.dot(place, query, preferred_element_type=F32).astype(BF16)
    number = neighbors_ref[...]
    coded = ((number & 127) + 128) << (number >> 7)
    coded = coded.astype(F32).astype(BF16)
    spread = lax.dot_general(place, coded, NT, preferred_element_type=F32).astype(BF16)
    filler = jnp.zeros((slot_count, send_ref.shape[1] - width - neighbor_count), BF16)
    send_ref[:, width:] = jnp.concatenate([spread, filler], axis=1)


def count_kernel(neighbor_count, received_ref, logcount_ref, low_ref, digit_ref):
    slot_count = logcount_ref.shape[1]
    width = received_ref.shape[1] - LANES
    coded = received_ref[:, width:].astype(F32)
    for block in range(slot_count // LANES):
        part = jnp.transpose(coded[block * LANES : (block + 1) * LANES])[:neighbor_count]
        high = jnp.zeros(part.shape, jnp.int32)
        for power in range(1, 8):
            high += (part >= float(128 << power)).astype(jnp.int32)
        value = part.astype(jnp.int32)
        low_ref[block] = (value >> high) - 128
        digit_ref[block] = jnp.int32(1) << (4 * high)

    def one(step, carry):
        block, half = step // 2, step % 2
        base = half * 64
        lanes = pl.ds(pl.multiple_of(block * LANES, LANES), LANES)
        rows = lax.broadcasted_iota(jnp.int32, (64, LANES), 0) + base
        even = jnp.zeros((64, LANES), jnp.int32)
        odd = jnp.zeros((64, LANES), jnp.int32)
        for first in range(0, neighbor_count, 13):
            total = jnp.zeros((64, LANES), jnp.int32)
            for k in range(first, min(first + 13, neighbor_count)):
                same = low_ref[block, k : k + 1, :] == rows
                total = total + jnp.where(same, digit_ref[block, k : k + 1, :], 0)
            even = even + (total & 0x0F0F0F0F)
            odd = odd + ((total >> 4) & 0x0F0F0F0F)
        for high in range(8):
            field = ((odd if high % 2 else even) >> (8 * (high // 2))) & 0xFF
            logs = jnp.where(field > 0, jnp.log2(field.astype(F32)), ABSENT)
            target = pl.ds(pl.multiple_of(high * LANES + base, 64), 64)
            logcount_ref[target, lanes] = logs
        return carry

    lax.fori_loop(0, slot_count // LANES * 2, one, 0)


def join_kernel(*refs):
    joined_ref = refs[-1]
    rows = refs[0].shape[0]
    for step, ref in enumerate(refs[:-1]):
        joined_ref[step * rows : (step + 1) * rows, :] = ref[...]


def attend_kernel(
    rows_held,
    query_ref,
    logcount_ref,
    own_ref,
    beside_ref,
    across_ref,
    slant_ref,
    w_key_ref,
    w_value_ref,
    mixed_ref,
    token_ref,
    key_ref,
    value_ref,
):
    slot_count, width = mixed_ref.shape
    head_width = width // HEADS
    place = lax.axis_index("shard")
    chips = token_ref.shape[0] // (2 * rows_held)
    for flip, ref in ((0, own_ref), (2, beside_ref), (1, across_ref), (3, slant_ref)):
        holder = jnp.bitwise_xor(place, flip)
        for step in range(chips // 2):
            origin = lax.rem(holder - 4 * step + 2 * chips, 2 * chips)
            target = pl.ds(pl.multiple_of(origin * rows_held, rows_held), rows_held)
            token_ref[target, :] = ref[step * rows_held : (step + 1) * rows_held, :]
    tokens = token_ref[...]
    key_ref[...] = jnp.dot(tokens, w_key_ref[...], preferred_element_type=F32).astype(BF16)
    value_ref[...] = lax.dot_general(
        w_value_ref[...], tokens, (((0,), (1,)), ((), ())), preferred_element_type=F32
    ).astype(BF16)
    factor = head_width ** (-0.5) * math.log2(math.e)
    size, chunk = 128, 256
    for block in range(slot_count // size):
        rows = slice(block * size, (block + 1) * size)
        for head in range(HEADS):
            columns = slice(head * head_width, (head + 1) * head_width)
            peak = jnp.full((1, size), 2 * ABSENT, F32)
            total = jnp.zeros((1, size), F32)
            mixed = jnp.zeros((head_width, size), F32)
            for first in range(0, key_ref.shape[0], chunk):
                part = slice(first, first + chunk)
                scores = lax.dot_general(
                    key_ref[part, columns], query_ref[rows, columns], NT, preferred_element_type=F32
                )
                scores = scores * factor + logcount_ref[part, rows]
                higher = jnp.maximum(peak, jnp.max(scores, axis=0, keepdims=True))
                raised = jnp.exp2(scores - higher)
                shrink = jnp.exp2(peak - higher)
                total = total * shrink + jnp.sum(raised, axis=0, keepdims=True)
                mixed = mixed * shrink + jnp.dot(
                    value_ref[columns, part], raised.astype(BF16), preferred_element_type=F32
                )
                peak = higher
            mixed_ref[rows, columns] = jnp.transpose(mixed / total).astype(BF16)


def finish_kernel(
    region_count,
    capacity,
    feats_ref,
    region_ref,
    returned_ref,
    w_out_ref,
    gain_ref,
    w_up_ref,
    w_down_ref,
    refined_ref,
):
    rows = feats_ref.shape[0]
    slot_count = region_count * capacity
    slot_row = slots_of(region_ref[...], region_count, capacity)
    slot_column = jnp.transpose(jnp.broadcast_to(slot_row, (LANES, rows)))
    pick = jnp.concatenate(
        [
            (lax.broadcasted_iota(jnp.int32, (rows, LANES), 1) + first).astype(F32) == slot_column
            for first in range(0, slot_count, LANES)
        ],
        axis=1,
    ).astype(BF16)
    mixed = jnp.dot(pick, returned_ref[...], preferred_element_type=F32).astype(BF16)
    resid = feats_ref[...].astype(F32) + jnp.dot(
        mixed, w_out_ref[...], preferred_element_type=F32
    )
    meansq = jnp.mean(resid * resid, axis=1, keepdims=True)
    normed = (resid * lax.rsqrt(meansq + 1e-05) * gain_ref[...]).astype(BF16)
    hidden = jax.nn.gelu(
        jnp.dot(normed, w_up_ref[...], preferred_element_type=F32), approximate=True
    ).astype(BF16)
    refined_ref[...] = (
        resid + jnp.dot(hidden, w_down_ref[...], preferred_element_type=F32)
    ).astype(BF16)


def params(mebibytes):
    return pltpu.CompilerParams(vmem_limit_bytes=mebibytes << 20)


def on_device(
    query_feats,
    query_region,
    neighbors,
    latents,
    w_query,
    w_key,
    w_value,
    w_out,
    norm_gain,
    w_up,
    w_down,
):
    region_count = lax.axis_size("region")
    shard_count = lax.axis_size("shard")
    chips = shard_count // 2
    query_count, width = query_feats.shape
    neighbor_count = neighbors.shape[1]
    capacity = min(query_count, 2 * query_count // region_count)
    slot_count = region_count * capacity
    wide = width + LANES
    table_rows = latents.shape[0] * shard_count
    region_row = query_region.reshape(1, query_count)

    def swap(flip):
        return [(place, place ^ flip) for place in range(shard_count)]

    pieces = [
        lax.ppermute(
            latents, "shard", [(place, (place + 4 * step) % shard_count) for place in range(shard_count)]
        )
        for step in range(1, chips // 2)
    ]
    send, held = pl.pallas_call(
        functools.partial(pack_kernel, region_count, capacity),
        grid=(1,),
        out_shape=[
            jax.ShapeDtypeStruct((slot_count, wide), BF16),
            jax.ShapeDtypeStruct(latents.shape, BF16),
        ],
        in_specs=[
            pl.BlockSpec((query_count, width), lambda i: (0, 0)),
            pl.BlockSpec((1, query_count), lambda i: (0, 0)),
            pl.BlockSpec((neighbor_count, query_count), lambda i: (0, 0)),
            pl.BlockSpec((width, width), lambda i: (0, 0)),
            pl.BlockSpec(latents.shape, lambda i: (0, 0)),
        ],
        out_specs=[pl.BlockSpec((slot_count, wide), lambda i: (0, 0)), VMEM],
        compiler_params=params(56),
        name="pack",
    )(query_feats, region_row, neighbors.T, w_query, latents)
    received = lax.all_to_all(
        send.reshape(region_count, capacity, wide), "region", split_axis=0, concat_axis=0, tiled=True
    ).reshape(slot_count, wide)
    own = pl.pallas_call(
        join_kernel,
        out_shape=jax.ShapeDtypeStruct(((len(pieces) + 1) * latents.shape[0], width), BF16),
        in_specs=[VMEM] * (len(pieces) + 1),
        out_specs=VMEM,
        compiler_params=params(4),
        cost_estimate=pl.CostEstimate(flops=10**11, bytes_accessed=0, transcendentals=0),
        name="join",
    )(held, *pieces)
    beside = lax.ppermute(own, "shard", swap(2))
    across = lax.ppermute(own, "shard", swap(1))
    slant = lax.ppermute(beside, "shard", swap(1))
    logcount = pl.pallas_call(
        functools.partial(count_kernel, neighbor_count),
        out_shape=jax.ShapeDtypeStruct((table_rows, slot_count), F32),
        in_specs=[VMEM],
        out_specs=VMEM,
        scratch_shapes=[
            pltpu.VMEM((slot_count // LANES, neighbor_count, LANES), jnp.int32),
            pltpu.VMEM((slot_count // LANES, neighbor_count, LANES), jnp.int32),
        ],
        compiler_params=params(8),
        name="count",
    )(received)
    mixed = pl.pallas_call(
        functools.partial(attend_kernel, latents.shape[0]),
        out_shape=jax.ShapeDtypeStruct((slot_count, width), BF16),
        in_specs=[VMEM] * 8,
        out_specs=VMEM,
        scratch_shapes=[
            pltpu.VMEM((table_rows, width), BF16),
            pltpu.VMEM((table_rows, width), BF16),
            pltpu.VMEM((width, table_rows), BF16),
        ],
        compiler_params=params(24),
        name="attend",
    )(received, logcount, own, beside, across, slant, w_key, w_value)
    returned = lax.all_to_all(
        mixed.reshape(region_count, capacity, width), "region", split_axis=0, concat_axis=0, tiled=True
    ).reshape(slot_count, width)
    return pl.pallas_call(
        functools.partial(finish_kernel, region_count, capacity),
        out_shape=jax.ShapeDtypeStruct((query_count, width), BF16),
        in_specs=[VMEM] * 7,
        out_specs=VMEM,
        compiler_params=params(24),
        name="finish",
    )(query_feats, region_row, returned, w_out, norm_gain.reshape(1, width), w_up, w_down)


def solution(mesh):
    in_specs = (P(("region", "shard"), None),) * 4 + (P(),) * 7
    out_specs = P(("region", "shard"), None)
    return jax.shard_map(
        on_device, mesh=mesh, in_specs=in_specs, out_specs=out_specs, check_vma=False
    )
```

```python
import functools
import math

import jax
import jax.numpy as jnp
from jax import lax
from jax.experimental import pallas as pl
from jax.experimental.pallas import tpu as pltpu
from jax.sharding import PartitionSpec as P

HEADS = 4
LANES = 128
ABSENT = -1e30
F32 = jnp.float32
BF16 = jnp.bfloat16
VMEM = pl.BlockSpec(memory_space=pltpu.VMEM)
NT = (((1,), (1,)), ((), ()))


def slots_of(region_row, region_count, capacity):
    rows = region_row.shape[1]
    onehot = (lax.broadcasted_iota(jnp.int32, (region_count, rows), 0) == region_row).astype(F32)
    earlier_than = lax.broadcasted_iota(jnp.int32, (rows, rows), 0) < lax.broadcasted_iota(
        jnp.int32, (rows, rows), 1
    )
    earlier = jnp.dot(onehot.astype(BF16), earlier_than.astype(BF16), preferred_element_type=F32)
    rank = jnp.sum(earlier * onehot, axis=0, keepdims=True)
    return region_row.astype(F32) * float(capacity) + rank


def pack_kernel(
    region_count,
    capacity,
    feats_hbm,
    region_hbm,
    neighbors_hbm,
    w_query_hbm,
    send_ref,
    feats_ref,
    region_ref,
    neighbors_ref,
    w_query_ref,
    arrived,
):
    sources = (region_hbm, neighbors_hbm, feats_hbm, w_query_hbm)
    targets = (region_ref, neighbors_ref, feats_ref, w_query_ref)
    copies = [
        pltpu.make_async_copy(source, target, arrived.at[number])
        for number, (source, target) in enumerate(zip(sources, targets))
    ]
    for copy in copies:
        copy.start()
    slot_count = region_count * capacity
    rows, width = feats_ref.shape
    copies[0].wait()
    slot_row = slots_of(region_ref[...], region_count, capacity)
    place = (
        lax.broadcasted_iota(jnp.int32, (slot_count, rows), 0).astype(F32) == slot_row
    ).astype(BF16)
    copies[1].wait()
    number = neighbors_ref[...]
    coded = ((number & 127) + 128) << (number >> 7)
    coded = coded.astype(F32).astype(BF16)
    spread = lax.dot_general(place, coded, NT, preferred_element_type=F32)
    spread = spread.reshape(region_count, capacity, spread.shape[1])
    half = capacity // 2
    spread = jnp.concatenate([spread[:, :half], spread[:, half:]], axis=2)
    send_ref[:, width // LANES * capacity :, :] = spread.astype(BF16)
    copies[2].wait()
    copies[3].wait()
    query = jnp.dot(feats_ref[...], w_query_ref[...], preferred_element_type=F32).astype(BF16)
    placed = jnp.dot(place, query, preferred_element_type=F32).astype(BF16)
    for head in range(width // LANES):
        send_ref[:, head * capacity : (head + 1) * capacity, :] = placed[
            :, head * LANES : (head + 1) * LANES
        ].reshape(region_count, capacity, LANES)


def count_kernel(neighbor_count, received_ref, logcount_ref, low_ref, digit_ref):
    slot_count = logcount_ref.shape[3]
    sources, rows, _ = received_ref.shape
    half = slot_count // sources // 2
    coded = received_ref[:, rows - half :, :].astype(F32).reshape(sources * half, LANES)
    blocks = slot_count // LANES
    for pair in range(blocks // 2):
        both = jnp.transpose(coded[pair * LANES : (pair + 1) * LANES])
        for side in range(2):
            part = both[side * neighbor_count : (side + 1) * neighbor_count]
            high = jnp.zeros(part.shape, jnp.int32)
            for power in range(1, 8):
                high += (part >= float(128 << power)).astype(jnp.int32)
            number = (high - 1) * 128 + (part.astype(jnp.int32) >> high)
            low_ref[side * (blocks // 2) + pair] = number & 63
            digit_ref[side * (blocks // 2) + pair] = jnp.int32(1) << (2 * (number >> 6))

    size = 32

    def one(step, carry):
        block, base = step // 2, step % 2 * size
        lanes = pl.ds(pl.multiple_of(block * LANES, LANES), LANES)
        inside = pl.ds(pl.multiple_of(base, size), size)
        numbers = lax.broadcasted_iota(jnp.int32, (size, LANES), 0) + base
        wide = [0, 0, 0, 0]
        for first in range(0, neighbor_count, 15):
            last = min(first + 15, neighbor_count)
            middle = [0, 0]
            for start in range(first, last, 3):
                narrow = 0
                for k in range(start, min(start + 3, last)):
                    same = low_ref[block, k : k + 1, :] == numbers
                    narrow = narrow + jnp.where(same, digit_ref[block, k : k + 1, :], 0)
                middle[0] = middle[0] + (narrow & 0x33333333)
                middle[1] = middle[1] + ((narrow >> 2) & 0x33333333)
            for odd in range(2):
                wide[odd] = wide[odd] + (middle[odd] & 0x0F0F0F0F)
                wide[2 + odd] = wide[2 + odd] + ((middle[odd] >> 4) & 0x0F0F0F0F)
        for digit in range(16):
            count = (wide[digit % 4] >> (8 * (digit // 4))) & 0xFF
            logs = jnp.maximum(jnp.log2(count.astype(F32)), ABSENT)
            logcount_ref[digit // 2, digit % 2, inside, lanes] = logs
        return carry

    lax.fori_loop(0, blocks * 2, one, 0)


def join_kernel(*refs):
    joined_ref = refs[-1]
    first = 0
    for ref in refs[:-1]:
        rows = ref.shape[0]
        joined_ref[first : first + rows, :] = ref[...]
        first += rows


def attend_kernel(
    first_part,
    rows_held,
    received_ref,
    logcount_ref,
    table_ref,
    table_more_ref,
    w_key_ref,
    w_value_ref,
    *refs,
):
    if first_part:
        mixed_out_ref, stats_out_ref, token_ref, key_ref, value_ref = refs
        sources, capacity = received_ref.shape[0], received_ref.shape[1] * 2 // (2 * HEADS + 1)
        width = w_key_ref.shape[1]
    else:
        mixed_in_ref, stats_in_ref, mixed_ref, token_ref, key_ref, value_ref = refs
        sources, capacity, width = mixed_ref.shape
    head_width = width // HEADS
    place = lax.axis_index("shard")
    chips = token_ref.shape[0] // rows_held
    chip, core = place // 2, place % 2
    if not first_part:
        core = 1 - core
    skip = 2 + 4 * core
    for step, offset in enumerate((0, 4, 1, 5, 7, 3, skip, skip + 4)):
        origin = lax.rem(chip + offset, chips)
        target = pl.ds(pl.multiple_of(origin * rows_held, rows_held), rows_held)
        ref, row = (table_ref, step) if step < 2 else (table_more_ref, step - 2)
        token_ref[target, :] = ref[row * rows_held : (row + 1) * rows_held, :]
    tokens = token_ref[...]
    key_ref[...] = jnp.dot(tokens, w_key_ref[...], preferred_element_type=F32).astype(BF16)
    value_ref[...] = lax.dot_general(
        w_value_ref[...], tokens, (((0,), (1,)), ((), ())), preferred_element_type=F32
    ).astype(BF16)
    factor = head_width ** (-0.5) * math.log2(math.e)
    half, chunk = capacity // 2, 256
    group = LANES // half
    for block in range(sources * capacity // LANES):
        side, first_source = divmod(block * group, sources)
        senders = slice(first_source, first_source + group)
        lanes = slice(block * LANES, (block + 1) * LANES)
        for head in range(HEADS):
            columns = slice(head * head_width, (head + 1) * head_width)
            top = head * capacity + side * half
            query = received_ref[senders, top : top + half, :].reshape(LANES, head_width)
            number = block * HEADS + head
            if first_part:
                peak = jnp.full((1, LANES), 2 * ABSENT, F32)
                total = jnp.zeros((1, LANES), F32)
                mixed = jnp.zeros((head_width, LANES), F32)
            else:
                peak = stats_in_ref[number, 0:1, :]
                total = stats_in_ref[number, 1:2, :]
                mixed = mixed_in_ref[number]
            for first in range(0, key_ref.shape[0], chunk):
                part = slice(first, first + chunk)
                holders = slice(first // rows_held, (first + chunk) // rows_held)
                scores = lax.dot_general(
                    key_ref[part, columns], query, NT, preferred_element_type=F32
                )
                logcount = logcount_ref[holders, core, :, lanes].reshape(chunk, LANES)
                scores = scores * factor + logcount
                higher = jnp.maximum(peak, jnp.max(scores, axis=0, keepdims=True))
                raised = jnp.exp2(scores - higher)
                shrink = jnp.exp2(peak - higher)
                total = total * shrink + jnp.sum(raised, axis=0, keepdims=True)
                mixed = mixed * shrink + jnp.dot(
                    value_ref[columns, part], raised.astype(BF16), preferred_element_type=F32
                )
                peak = higher
            if first_part:
                mixed_out_ref[number] = mixed
                stats_out_ref[number, 0:1, :] = peak
                stats_out_ref[number, 1:2, :] = total
            else:
                mixed_ref[senders, side * half : (side + 1) * half, columns] = (
                    jnp.transpose(mixed / total).astype(BF16).reshape(group, half, head_width)
                )


def pick_kernel(region_count, capacity, region_ref, after_ref, pick_ref):
    rows, slot_count = pick_ref.shape
    slot_row = slots_of(region_ref[...], region_count, capacity)
    slot_column = jnp.transpose(jnp.broadcast_to(slot_row, (LANES, rows)))
    pick_ref[...] = jnp.concatenate(
        [
            (lax.broadcasted_iota(jnp.int32, (rows, LANES), 1) + first).astype(F32) == slot_column
            for first in range(0, slot_count, LANES)
        ],
        axis=1,
    ).astype(BF16)


def finish_kernel(
    feats_ref,
    pick_ref,
    returned_ref,
    w_out_ref,
    gain_ref,
    w_up_ref,
    w_down_ref,
    refined_ref,
):
    mixed = jnp.dot(pick_ref[...], returned_ref[...], preferred_element_type=F32).astype(BF16)
    resid = feats_ref[...].astype(F32) + jnp.dot(
        mixed, w_out_ref[...], preferred_element_type=F32
    )
    meansq = jnp.mean(resid * resid, axis=1, keepdims=True)
    normed = (resid * lax.rsqrt(meansq + 1e-05) * gain_ref[...]).astype(BF16)
    hidden = jax.nn.gelu(
        jnp.dot(normed, w_up_ref[...], preferred_element_type=F32), approximate=True
    ).astype(BF16)
    refined_ref[...] = (
        resid + jnp.dot(hidden, w_down_ref[...], preferred_element_type=F32)
    ).astype(BF16)


def params(mebibytes):
    return pltpu.CompilerParams(vmem_limit_bytes=mebibytes << 20)


def on_device(
    query_feats,
    query_region,
    neighbors,
    latents,
    w_query,
    w_key,
    w_value,
    w_out,
    norm_gain,
    w_up,
    w_down,
):
    region_count = lax.axis_size("region")
    shard_count = lax.axis_size("shard")
    chips = shard_count // 2
    query_count, width = query_feats.shape
    neighbor_count = neighbors.shape[1]
    capacity = min(query_count, 2 * query_count // region_count)
    slot_count = region_count * capacity
    table_rows = latents.shape[0] * chips
    region_row = query_region.reshape(1, query_count)
    payload = (region_count, width // LANES * capacity + capacity // 2, LANES)

    def fetch(table, chip_offset, other_offset=None):
        steps = (chip_offset, chip_offset if other_offset is None else other_offset)
        pairs = [
            ((chip + steps[core]) % chips * 2 + core, chip * 2 + core)
            for chip in range(chips)
            for core in range(2)
        ]
        return lax.ppermute(table, "shard", pairs)

    def swap(table):
        return lax.ppermute(table, "shard", [(place, place ^ 1) for place in range(shard_count)])

    def join(pieces, flops, name):
        rows = sum(piece.shape[0] for piece in pieces)
        return pl.pallas_call(
            join_kernel,
            out_shape=jax.ShapeDtypeStruct((rows, width), BF16),
            in_specs=[VMEM] * len(pieces),
            out_specs=VMEM,
            compiler_params=params(4),
            cost_estimate=pl.CostEstimate(flops=flops, bytes_accessed=0, transcendentals=0),
            name=name,
        )(*pieces)

    opposite = fetch(latents, 4)
    send = pl.pallas_call(
        functools.partial(pack_kernel, region_count, capacity),
        out_shape=jax.ShapeDtypeStruct(payload, BF16),
        in_specs=[pl.BlockSpec(memory_space=pl.ANY)] * 4,
        out_specs=VMEM,
        scratch_shapes=[
            pltpu.VMEM((query_count, width), BF16),
            pltpu.VMEM((1, query_count), jnp.int32),
            pltpu.VMEM((neighbor_count, query_count), jnp.int32),
            pltpu.VMEM((width, width), BF16),
            pltpu.SemaphoreType.DMA((4,)),
        ],
        compiler_params=params(56),
        name="pack",
    )(query_feats, region_row, neighbors.T, w_query)
    received = lax.all_to_all(send, "region", split_axis=0, concat_axis=0, tiled=True)
    near = join([latents, opposite], 10**11, "join_near")
    pick = pl.pallas_call(
        functools.partial(pick_kernel, region_count, capacity),
        out_shape=jax.ShapeDtypeStruct((query_count, slot_count), BF16),
        in_specs=[VMEM] * 2,
        out_specs=VMEM,
        compiler_params=params(4),
        cost_estimate=pl.CostEstimate(flops=10**10, bytes_accessed=0, transcendentals=0),
        name="pick",
    )(region_row, near)
    received, pick = lax.optimization_barrier((received, pick))
    logcount = pl.pallas_call(
        functools.partial(count_kernel, neighbor_count),
        out_shape=jax.ShapeDtypeStruct((chips, 2, latents.shape[0], slot_count), F32),
        in_specs=[VMEM],
        out_specs=VMEM,
        scratch_shapes=[
            pltpu.VMEM((slot_count // LANES, neighbor_count, LANES), jnp.int32),
            pltpu.VMEM((slot_count // LANES, neighbor_count, LANES), jnp.int32),
        ],
        compiler_params=params(8),
        name="count",
    )(received)
    arrivals = [fetch(near, 1), fetch(near, -1), fetch(near, 2, -2)]
    arrivals, logcount = lax.optimization_barrier((arrivals, logcount))
    near_more = join(arrivals, 0, "join_more")
    far = swap(near)
    far_more = swap(near_more)
    scratch = [
        pltpu.VMEM((table_rows, width), BF16),
        pltpu.VMEM((table_rows, width), BF16),
        pltpu.VMEM((width, table_rows), BF16),
    ]
    groups = slot_count // LANES * HEADS
    sums = pl.pallas_call(
        functools.partial(attend_kernel, True, latents.shape[0]),
        out_shape=[
            jax.ShapeDtypeStruct((groups, width // HEADS, LANES), F32),
            jax.ShapeDtypeStruct((groups, 8, LANES), F32),
        ],
        in_specs=[VMEM] * 6,
        out_specs=[VMEM] * 2,
        scratch_shapes=scratch,
        compiler_params=params(16),
        cost_estimate=pl.CostEstimate(flops=10**10, bytes_accessed=0, transcendentals=0),
        name="attend_near",
    )(received, logcount, near, near_more, w_key, w_value)
    mixed = pl.pallas_call(
        functools.partial(attend_kernel, False, latents.shape[0]),
        out_shape=jax.ShapeDtypeStruct((region_count, capacity, width), BF16),
        in_specs=[VMEM] * 8,
        out_specs=VMEM,
        scratch_shapes=scratch,
        compiler_params=params(16),
        name="attend_far",
    )(received, logcount, far, far_more, w_key, w_value, *sums)
    returned = lax.all_to_all(
        mixed, "region", split_axis=0, concat_axis=0, tiled=True
    ).reshape(slot_count, width)
    return pl.pallas_call(
        finish_kernel,
        out_shape=jax.ShapeDtypeStruct((query_count, width), BF16),
        in_specs=[VMEM] * 7,
        out_specs=VMEM,
        compiler_params=params(24),
        name="finish",
    )(query_feats, pick, returned, w_out, norm_gain.reshape(1, width), w_up, w_down)


def solution(mesh):
    in_specs = (P(("region", "shard"), None),) * 4 + (P(),) * 7
    out_specs = P(("region", "shard"), None)
    return jax.shard_map(
        on_device, mesh=mesh, in_specs=in_specs, out_specs=out_specs, check_vma=False
    )
```

```python
import functools
import math

import jax
import jax.numpy as jnp
from jax import lax
from jax.experimental import pallas as pl
from jax.experimental.pallas import tpu as pltpu
from jax.sharding import PartitionSpec as P

HEADS = 4
LANES = 128
ABSENT = -1e30
F32 = jnp.float32
BF16 = jnp.bfloat16
VMEM = pl.BlockSpec(memory_space=pltpu.VMEM)
NT = (((1,), (1,)), ((), ()))


def slots_of(region_row, region_count, capacity):
    rows = region_row.shape[1]
    onehot = (lax.broadcasted_iota(jnp.int32, (region_count, rows), 0) == region_row).astype(F32)
    earlier_than = lax.broadcasted_iota(jnp.int32, (rows, rows), 0) < lax.broadcasted_iota(
        jnp.int32, (rows, rows), 1
    )
    earlier = jnp.dot(onehot.astype(BF16), earlier_than.astype(BF16), preferred_element_type=F32)
    rank = jnp.sum(earlier * onehot, axis=0, keepdims=True)
    return region_row.astype(F32) * float(capacity) + rank


def pack_kernel(region_count, capacity, early_turn, *refs):
    feats_hbm, region_hbm, neighbors_hbm, w_query_hbm = refs[:4]
    send_hbm, feats_ref, region_ref, neighbors_ref, w_query_ref, send_ref, arrived, left = refs[-8:]
    early = lax.axis_index("shard") < lax.axis_size("shard") * 3 // 8

    @pl.when(early if early_turn else jnp.logical_not(early))
    def _():
        sources = (region_hbm, neighbors_hbm, feats_hbm, w_query_hbm)
        targets = (region_ref, neighbors_ref, feats_ref, w_query_ref)
        copies = [
            pltpu.make_async_copy(source, target, arrived.at[number])
            for number, (source, target) in enumerate(zip(sources, targets))
        ]
        for copy in copies:
            copy.start()
        slot_count = region_count * capacity
        rows, width = feats_ref.shape
        copies[0].wait()
        slot_row = slots_of(region_ref[...], region_count, capacity)
        place = (
            lax.broadcasted_iota(jnp.int32, (slot_count, rows), 0).astype(F32) == slot_row
        ).astype(BF16)
        copies[1].wait()
        number = neighbors_ref[...]
        coded = ((number & 127) + 128) << (number >> 7)
        coded = coded.astype(F32).astype(BF16)
        spread = lax.dot_general(place, coded, NT, preferred_element_type=F32)
        spread = spread.reshape(region_count, capacity, spread.shape[1])
        half = capacity // 2
        spread = jnp.concatenate([spread[:, :half], spread[:, half:]], axis=2)
        send_ref[:, width // LANES * capacity :, :] = spread.astype(BF16)
        copies[2].wait()
        copies[3].wait()
        query = jnp.dot(feats_ref[...], w_query_ref[...], preferred_element_type=F32)
        placed = jnp.dot(place, query.astype(BF16), preferred_element_type=F32).astype(BF16)
        for head in range(width // LANES):
            send_ref[:, head * capacity : (head + 1) * capacity, :] = placed[
                :, head * LANES : (head + 1) * LANES
            ].reshape(region_count, capacity, LANES)
        leaving = pltpu.make_async_copy(send_ref, send_hbm, left)
        leaving.start()
        leaving.wait()


def count_kernel(neighbor_count, received_ref, logcount_ref, low_ref, digit_ref):
    slot_count = logcount_ref.shape[3]
    sources, rows, _ = received_ref.shape
    half = slot_count // sources // 2
    coded = received_ref[:, rows - half :, :].astype(F32).reshape(sources * half, LANES)
    blocks = slot_count // LANES
    for pair in range(blocks // 2):
        both = jnp.transpose(coded[pair * LANES : (pair + 1) * LANES])
        for side in range(2):
            part = both[side * neighbor_count : (side + 1) * neighbor_count]
            high = jnp.zeros(part.shape, jnp.int32)
            for power in range(1, 8):
                high += (part >= float(128 << power)).astype(jnp.int32)
            number = (high - 1) * 128 + (part.astype(jnp.int32) >> high)
            low_ref[side * (blocks // 2) + pair] = number & 63
            digit_ref[side * (blocks // 2) + pair] = jnp.int32(1) << (2 * (number >> 6))

    size = 32

    def one(step, carry):
        block, base = step // 2, step % 2 * size
        lanes = pl.ds(pl.multiple_of(block * LANES, LANES), LANES)
        inside = pl.ds(pl.multiple_of(base, size), size)
        numbers = lax.broadcasted_iota(jnp.int32, (size, LANES), 0) + base
        wide = [0, 0, 0, 0]
        for first in range(0, neighbor_count, 15):
            last = min(first + 15, neighbor_count)
            middle = [0, 0]
            for start in range(first, last, 3):
                narrow = 0
                for k in range(start, min(start + 3, last)):
                    same = low_ref[block, k : k + 1, :] == numbers
                    narrow = narrow + jnp.where(same, digit_ref[block, k : k + 1, :], 0)
                middle[0] = middle[0] + (narrow & 0x33333333)
                middle[1] = middle[1] + ((narrow >> 2) & 0x33333333)
            for odd in range(2):
                wide[odd] = wide[odd] + (middle[odd] & 0x0F0F0F0F)
                wide[2 + odd] = wide[2 + odd] + ((middle[odd] >> 4) & 0x0F0F0F0F)
        for digit in range(16):
            count = (wide[digit % 4] >> (8 * (digit // 4))) & 0xFF
            logs = jnp.maximum(jnp.log2(count.astype(F32)), ABSENT)
            logcount_ref[digit // 2, digit % 2, inside, lanes] = logs
        return carry

    lax.fori_loop(0, blocks * 2, one, 0)


def join_kernel(*refs):
    joined_ref = refs[-1]
    first = 0
    for ref in refs[:-1]:
        rows = ref.shape[0]
        joined_ref[first : first + rows, :] = ref[...]
        first += rows


def attend_kernel(
    first_part,
    rows_held,
    received_ref,
    logcount_ref,
    table_ref,
    table_more_ref,
    w_key_ref,
    w_value_ref,
    *refs,
):
    if first_part:
        mixed_out_ref, stats_out_ref, token_ref, key_ref, value_ref = refs
        sources, capacity = received_ref.shape[0], received_ref.shape[1] * 2 // (2 * HEADS + 1)
        width = w_key_ref.shape[1]
    else:
        mixed_in_ref, stats_in_ref, mixed_ref, token_ref, key_ref, value_ref = refs
        sources, capacity, width = mixed_ref.shape
    head_width = width // HEADS
    place = lax.axis_index("shard")
    chips = token_ref.shape[0] // rows_held
    chip, core = place // 2, place % 2
    if not first_part:
        core = 1 - core
    skip = 2 + 4 * core
    for step, offset in enumerate((0, 4, 1, 5, 7, 3, skip, skip + 4)):
        origin = lax.rem(chip + offset, chips)
        target = pl.ds(pl.multiple_of(origin * rows_held, rows_held), rows_held)
        ref, row = (table_ref, step) if step < 2 else (table_more_ref, step - 2)
        token_ref[target, :] = ref[row * rows_held : (row + 1) * rows_held, :]
    tokens = token_ref[...]
    key_ref[...] = jnp.dot(tokens, w_key_ref[...], preferred_element_type=F32).astype(BF16)
    value_ref[...] = lax.dot_general(
        w_value_ref[...], tokens, (((0,), (1,)), ((), ())), preferred_element_type=F32
    ).astype(BF16)
    factor = head_width ** (-0.5) * math.log2(math.e)
    half, chunk = capacity // 2, 256
    group = LANES // half
    for block in range(sources * capacity // LANES):
        side, first_source = divmod(block * group, sources)
        senders = slice(first_source, first_source + group)
        lanes = slice(block * LANES, (block + 1) * LANES)
        for head in range(HEADS):
            columns = slice(head * head_width, (head + 1) * head_width)
            top = head * capacity + side * half
            query = received_ref[senders, top : top + half, :].reshape(LANES, head_width)
            number = block * HEADS + head
            if first_part:
                peak = jnp.full((1, LANES), 2 * ABSENT, F32)
                total = jnp.zeros((1, LANES), F32)
                mixed = jnp.zeros((head_width, LANES), F32)
            else:
                peak = stats_in_ref[number, 0:1, :]
                total = stats_in_ref[number, 1:2, :]
                mixed = mixed_in_ref[number]
            for first in range(0, key_ref.shape[0], chunk):
                part = slice(first, first + chunk)
                holders = slice(first // rows_held, (first + chunk) // rows_held)
                scores = lax.dot_general(
                    key_ref[part, columns], query, NT, preferred_element_type=F32
                )
                logcount = logcount_ref[holders, core, :, lanes].reshape(chunk, LANES)
                scores = scores * factor + logcount
                higher = jnp.maximum(peak, jnp.max(scores, axis=0, keepdims=True))
                raised = jnp.exp2(scores - higher)
                shrink = jnp.exp2(peak - higher)
                total = total * shrink + jnp.sum(raised, axis=0, keepdims=True)
                mixed = mixed * shrink + jnp.dot(
                    value_ref[columns, part], raised.astype(BF16), preferred_element_type=F32
                )
                peak = higher
            if first_part:
                mixed_out_ref[number] = mixed
                stats_out_ref[number, 0:1, :] = peak
                stats_out_ref[number, 1:2, :] = total
            else:
                mixed_ref[senders, side * half : (side + 1) * half, columns] = (
                    jnp.transpose(mixed / total).astype(BF16).reshape(group, half, head_width)
                )


def pick_kernel(region_count, capacity, region_ref, after_ref, pick_ref):
    rows, slot_count = pick_ref.shape
    slot_row = slots_of(region_ref[...], region_count, capacity)
    slot_column = jnp.transpose(jnp.broadcast_to(slot_row, (LANES, rows)))
    pick_ref[...] = jnp.concatenate(
        [
            (lax.broadcasted_iota(jnp.int32, (rows, LANES), 1) + first).astype(F32) == slot_column
            for first in range(0, slot_count, LANES)
        ],
        axis=1,
    ).astype(BF16)


def finish_kernel(
    feats_ref,
    pick_ref,
    returned_ref,
    w_out_ref,
    gain_ref,
    w_up_ref,
    w_down_ref,
    refined_ref,
):
    mixed = jnp.dot(pick_ref[...], returned_ref[...], preferred_element_type=F32).astype(BF16)
    resid = feats_ref[...].astype(F32) + jnp.dot(
        mixed, w_out_ref[...], preferred_element_type=F32
    )
    meansq = jnp.mean(resid * resid, axis=1, keepdims=True)
    normed = (resid * lax.rsqrt(meansq + 1e-05) * gain_ref[...]).astype(BF16)
    hidden = jax.nn.gelu(
        jnp.dot(normed, w_up_ref[...], preferred_element_type=F32), approximate=True
    ).astype(BF16)
    refined_ref[...] = (
        resid + jnp.dot(hidden, w_down_ref[...], preferred_element_type=F32)
    ).astype(BF16)


def params(mebibytes):
    return pltpu.CompilerParams(vmem_limit_bytes=mebibytes << 20)


def on_device(
    query_feats,
    query_region,
    neighbors,
    latents,
    w_query,
    w_key,
    w_value,
    w_out,
    norm_gain,
    w_up,
    w_down,
):
    region_count = lax.axis_size("region")
    shard_count = lax.axis_size("shard")
    chips = shard_count // 2
    query_count, width = query_feats.shape
    neighbor_count = neighbors.shape[1]
    capacity = min(query_count, 2 * query_count // region_count)
    slot_count = region_count * capacity
    table_rows = latents.shape[0] * chips
    region_row = query_region.reshape(1, query_count)
    payload = (region_count, width // LANES * capacity + capacity // 2, LANES)

    def fetch(table, chip_offset, other_offset=None):
        steps = (chip_offset, chip_offset if other_offset is None else other_offset)
        pairs = [
            ((chip + steps[core]) % chips * 2 + core, chip * 2 + core)
            for chip in range(chips)
            for core in range(2)
        ]
        return lax.ppermute(table, "shard", pairs)

    def swap(table):
        return lax.ppermute(table, "shard", [(place, place ^ 1) for place in range(shard_count)])

    def join(pieces, flops, name):
        rows = sum(piece.shape[0] for piece in pieces)
        return pl.pallas_call(
            join_kernel,
            out_shape=jax.ShapeDtypeStruct((rows, width), BF16),
            in_specs=[VMEM] * len(pieces),
            out_specs=VMEM,
            compiler_params=params(4),
            cost_estimate=pl.CostEstimate(flops=flops, bytes_accessed=0, transcendentals=0),
            name=name,
        )(*pieces)

    def pack(early_turn, *begun):
        anywhere = pl.BlockSpec(memory_space=pl.ANY)
        return pl.pallas_call(
            functools.partial(pack_kernel, region_count, capacity, early_turn),
            out_shape=jax.ShapeDtypeStruct(payload, BF16),
            in_specs=[anywhere] * (4 + len(begun)),
            out_specs=anywhere,
            scratch_shapes=[
                pltpu.VMEM((query_count, width), BF16),
                pltpu.VMEM((1, query_count), jnp.int32),
                pltpu.VMEM((neighbor_count, query_count), jnp.int32),
                pltpu.VMEM((width, width), BF16),
                pltpu.VMEM(payload, BF16),
                pltpu.SemaphoreType.DMA((4,)),
                pltpu.SemaphoreType.DMA,
            ],
            input_output_aliases={4: 0} if begun else {},
            compiler_params=params(56),
            name="pack_early" if early_turn else "pack_late",
        )(query_feats, region_row, neighbors.T, w_query, *begun)

    begun, latents = lax.optimization_barrier((pack(True), latents))
    opposite = fetch(latents, 4)
    send = pack(False, begun)
    received = lax.all_to_all(send, "region", split_axis=0, concat_axis=0, tiled=True)
    near = join([latents, opposite], 10**11, "join_near")
    pick = pl.pallas_call(
        functools.partial(pick_kernel, region_count, capacity),
        out_shape=jax.ShapeDtypeStruct((query_count, slot_count), BF16),
        in_specs=[VMEM] * 2,
        out_specs=VMEM,
        compiler_params=params(4),
        cost_estimate=pl.CostEstimate(flops=10**10, bytes_accessed=0, transcendentals=0),
        name="pick",
    )(region_row, near)
    received, pick = lax.optimization_barrier((received, pick))
    logcount = pl.pallas_call(
        functools.partial(count_kernel, neighbor_count),
        out_shape=jax.ShapeDtypeStruct((chips, 2, latents.shape[0], slot_count), F32),
        in_specs=[VMEM],
        out_specs=VMEM,
        scratch_shapes=[
            pltpu.VMEM((slot_count // LANES, neighbor_count, LANES), jnp.int32),
            pltpu.VMEM((slot_count // LANES, neighbor_count, LANES), jnp.int32),
        ],
        compiler_params=params(8),
        name="count",
    )(received)
    arrivals = [fetch(near, 1), fetch(near, -1), fetch(near, 2, -2)]
    arrivals, logcount = lax.optimization_barrier((arrivals, logcount))
    near_more = join(arrivals, 0, "join_more")
    far = swap(near)
    far_more = swap(near_more)
    scratch = [
        pltpu.VMEM((table_rows, width), BF16),
        pltpu.VMEM((table_rows, width), BF16),
        pltpu.VMEM((width, table_rows), BF16),
    ]
    groups = slot_count // LANES * HEADS
    sums = pl.pallas_call(
        functools.partial(attend_kernel, True, latents.shape[0]),
        out_shape=[
            jax.ShapeDtypeStruct((groups, width // HEADS, LANES), F32),
            jax.ShapeDtypeStruct((groups, 8, LANES), F32),
        ],
        in_specs=[VMEM] * 6,
        out_specs=[VMEM] * 2,
        scratch_shapes=scratch,
        compiler_params=params(16),
        cost_estimate=pl.CostEstimate(flops=10**10, bytes_accessed=0, transcendentals=0),
        name="attend_near",
    )(received, logcount, near, near_more, w_key, w_value)
    mixed = pl.pallas_call(
        functools.partial(attend_kernel, False, latents.shape[0]),
        out_shape=jax.ShapeDtypeStruct((region_count, capacity, width), BF16),
        in_specs=[VMEM] * 8,
        out_specs=VMEM,
        scratch_shapes=scratch,
        compiler_params=params(16),
        name="attend_far",
    )(received, logcount, far, far_more, w_key, w_value, *sums)
    returned = lax.all_to_all(
        mixed, "region", split_axis=0, concat_axis=0, tiled=True
    ).reshape(slot_count, width)
    return pl.pallas_call(
        finish_kernel,
        out_shape=jax.ShapeDtypeStruct((query_count, width), BF16),
        in_specs=[VMEM] * 7,
        out_specs=VMEM,
        compiler_params=params(24),
        name="finish",
    )(query_feats, pick, returned, w_out, norm_gain.reshape(1, width), w_up, w_down)


def solution(mesh):
    in_specs = (P(("region", "shard"), None),) * 4 + (P(),) * 7
    out_specs = P(("region", "shard"), None)
    return jax.shard_map(
        on_device, mesh=mesh, in_specs=in_specs, out_specs=out_specs, check_vma=False
    )
```

```python
import functools
import math

import jax
import jax.numpy as jnp
from jax import lax
from jax.experimental import pallas as pl
from jax.experimental.pallas import tpu as pltpu
from jax.sharding import PartitionSpec as P

HEADS = 4
LANES = 128
ABSENT = -1e30
F32 = jnp.float32
BF16 = jnp.bfloat16
VMEM = pl.BlockSpec(memory_space=pltpu.VMEM)
NT = (((1,), (1,)), ((), ()))


def slots_of(region_row, region_count, capacity):
    rows = region_row.shape[1]
    onehot = (lax.broadcasted_iota(jnp.int32, (region_count, rows), 0) == region_row).astype(F32)
    earlier_than = lax.broadcasted_iota(jnp.int32, (rows, rows), 0) < lax.broadcasted_iota(
        jnp.int32, (rows, rows), 1
    )
    earlier = jnp.dot(onehot.astype(BF16), earlier_than.astype(BF16), preferred_element_type=F32)
    rank = jnp.sum(earlier * onehot, axis=0, keepdims=True)
    return region_row.astype(F32) * float(capacity) + rank


def pack_kernel(region_count, capacity, early_turn, *refs):
    feats_hbm, region_hbm, neighbors_hbm, w_query_hbm = refs[:4]
    send_hbm, feats_ref, region_ref, neighbors_ref, w_query_ref, send_ref, arrived, left = refs[-8:]
    early = lax.axis_index("shard") < lax.axis_size("shard") * 3 // 8

    @pl.when(early if early_turn else jnp.logical_not(early))
    def _():
        sources = (region_hbm, neighbors_hbm, feats_hbm, w_query_hbm)
        targets = (region_ref, neighbors_ref, feats_ref, w_query_ref)
        copies = [
            pltpu.make_async_copy(source, target, arrived.at[number])
            for number, (source, target) in enumerate(zip(sources, targets))
        ]
        for copy in copies:
            copy.start()
        slot_count = region_count * capacity
        rows, width = feats_ref.shape
        copies[0].wait()
        slot_row = slots_of(region_ref[...], region_count, capacity)
        place = (
            lax.broadcasted_iota(jnp.int32, (slot_count, rows), 0).astype(F32) == slot_row
        ).astype(BF16)
        copies[1].wait()
        number = neighbors_ref[...]
        coded = ((number & 127) + 128) << (number >> 7)
        coded = coded.astype(F32).astype(BF16)
        spread = lax.dot_general(place, coded, NT, preferred_element_type=F32)
        spread = spread.reshape(region_count, capacity, spread.shape[1])
        half = capacity // 2
        spread = jnp.concatenate([spread[:, :half], spread[:, half:]], axis=2)
        send_ref[:, width // LANES * capacity :, :] = spread.astype(BF16)
        copies[2].wait()
        copies[3].wait()
        query = jnp.dot(feats_ref[...], w_query_ref[...], preferred_element_type=F32)
        placed = jnp.dot(place, query.astype(BF16), preferred_element_type=F32).astype(BF16)
        for head in range(width // LANES):
            send_ref[:, head * capacity : (head + 1) * capacity, :] = placed[
                :, head * LANES : (head + 1) * LANES
            ].reshape(region_count, capacity, LANES)
        leaving = pltpu.make_async_copy(send_ref, send_hbm, left)
        leaving.start()
        leaving.wait()


def count_kernel(neighbor_count, received_ref, logcount_ref, low_ref, digit_ref):
    slot_count = logcount_ref.shape[3]
    sources, rows, _ = received_ref.shape
    half = slot_count // sources // 2
    coded = received_ref[:, rows - half :, :].astype(F32).reshape(sources * half, LANES)
    blocks = slot_count // LANES
    for pair in range(blocks // 2):
        both = jnp.transpose(coded[pair * LANES : (pair + 1) * LANES])
        for side in range(2):
            part = both[side * neighbor_count : (side + 1) * neighbor_count]
            high = jnp.zeros(part.shape, jnp.int32)
            for power in range(1, 8):
                high += (part >= float(128 << power)).astype(jnp.int32)
            number = (high - 1) * 128 + (part.astype(jnp.int32) >> high)
            low_ref[side * (blocks // 2) + pair] = number & 63
            digit_ref[side * (blocks // 2) + pair] = jnp.int32(1) << (2 * (number >> 6))

    size = 32

    def one(step, carry):
        block, base = step // 2, step % 2 * size
        lanes = pl.ds(pl.multiple_of(block * LANES, LANES), LANES)
        inside = pl.ds(pl.multiple_of(base, size), size)
        numbers = lax.broadcasted_iota(jnp.int32, (size, LANES), 0) + base
        wide = [0, 0, 0, 0]
        for first in range(0, neighbor_count, 15):
            last = min(first + 15, neighbor_count)
            middle = [0, 0]
            for start in range(first, last, 3):
                narrow = 0
                for k in range(start, min(start + 3, last)):
                    same = low_ref[block, k : k + 1, :] == numbers
                    narrow = narrow + jnp.where(same, digit_ref[block, k : k + 1, :], 0)
                middle[0] = middle[0] + (narrow & 0x33333333)
                middle[1] = middle[1] + ((narrow >> 2) & 0x33333333)
            for odd in range(2):
                wide[odd] = wide[odd] + (middle[odd] & 0x0F0F0F0F)
                wide[2 + odd] = wide[2 + odd] + ((middle[odd] >> 4) & 0x0F0F0F0F)
        for digit in range(16):
            count = (wide[digit % 4] >> (8 * (digit // 4))) & 0xFF
            logs = jnp.maximum(jnp.log2(count.astype(F32)), ABSENT)
            logcount_ref[digit // 2, digit % 2, inside, lanes] = logs
        return carry

    lax.fori_loop(0, blocks * 2, one, 0)


def join_kernel(*refs):
    joined_ref = refs[-1]
    first = 0
    for ref in refs[:-1]:
        rows = ref.shape[0]
        joined_ref[first : first + rows, :] = ref[...]
        first += rows


def attend_kernel(
    first_part,
    rows_held,
    received_ref,
    logcount_ref,
    table_ref,
    w_key_ref,
    w_value_ref,
    *refs,
):
    if first_part:
        mixed_out_ref, stats_out_ref, token_ref, key_ref, value_ref = refs
        sources, capacity = received_ref.shape[0], received_ref.shape[1] * 2 // (2 * HEADS + 1)
        width = w_key_ref.shape[1]
    else:
        mixed_in_ref, stats_in_ref, mixed_ref, token_ref, key_ref, value_ref = refs
        sources, capacity, width = mixed_ref.shape
    head_width = width // HEADS
    place = lax.axis_index("shard")
    chips = token_ref.shape[0] // rows_held
    chip, core = place // 2, place % 2
    if not first_part:
        core = 1 - core
    turn = 1 - 2 * (chip % 2)
    steps = (0, 3 * turn, 1, 1 - 3 * turn, -1, -1 - 3 * turn, 2 * turn, 5 * turn)
    for step, offset in enumerate(steps):
        origin = lax.rem(chip + offset + chips, chips)
        target = pl.ds(pl.multiple_of(origin * rows_held, rows_held), rows_held)
        token_ref[target, :] = table_ref[step * rows_held : (step + 1) * rows_held, :]
    tokens = token_ref[...]
    key_ref[...] = jnp.dot(tokens, w_key_ref[...], preferred_element_type=F32).astype(BF16)
    value_ref[...] = lax.dot_general(
        w_value_ref[...], tokens, (((0,), (1,)), ((), ())), preferred_element_type=F32
    ).astype(BF16)
    factor = head_width ** (-0.5) * math.log2(math.e)
    half, chunk = capacity // 2, 256
    group = LANES // half
    for block in range(sources * capacity // LANES):
        side, first_source = divmod(block * group, sources)
        senders = slice(first_source, first_source + group)
        lanes = slice(block * LANES, (block + 1) * LANES)
        for head in range(HEADS):
            columns = slice(head * head_width, (head + 1) * head_width)
            top = head * capacity + side * half
            query = received_ref[senders, top : top + half, :].reshape(LANES, head_width)
            number = block * HEADS + head
            if first_part:
                peak = jnp.full((1, LANES), 2 * ABSENT, F32)
                total = jnp.zeros((1, LANES), F32)
                mixed = jnp.zeros((head_width, LANES), F32)
            else:
                peak = stats_in_ref[number, 0:1, :]
                total = stats_in_ref[number, 1:2, :]
                mixed = mixed_in_ref[number]
            for first in range(0, key_ref.shape[0], chunk):
                part = slice(first, first + chunk)
                holders = slice(first // rows_held, (first + chunk) // rows_held)
                scores = lax.dot_general(
                    key_ref[part, columns], query, NT, preferred_element_type=F32
                )
                logcount = logcount_ref[holders, core, :, lanes].reshape(chunk, LANES)
                scores = scores * factor + logcount
                higher = jnp.maximum(peak, jnp.max(scores, axis=0, keepdims=True))
                raised = jnp.exp2(scores - higher)
                shrink = jnp.exp2(peak - higher)
                total = total * shrink + jnp.sum(raised, axis=0, keepdims=True)
                mixed = mixed * shrink + jnp.dot(
                    value_ref[columns, part], raised.astype(BF16), preferred_element_type=F32
                )
                peak = higher
            if first_part:
                mixed_out_ref[number] = mixed
                stats_out_ref[number, 0:1, :] = peak
                stats_out_ref[number, 1:2, :] = total
            else:
                mixed_ref[senders, side * half : (side + 1) * half, columns] = (
                    jnp.transpose(mixed / total).astype(BF16).reshape(group, half, head_width)
                )


def pick_kernel(region_count, capacity, region_ref, after_ref, pick_ref):
    rows, slot_count = pick_ref.shape
    slot_row = slots_of(region_ref[...], region_count, capacity)
    slot_column = jnp.transpose(jnp.broadcast_to(slot_row, (LANES, rows)))
    pick_ref[...] = jnp.concatenate(
        [
            (lax.broadcasted_iota(jnp.int32, (rows, LANES), 1) + first).astype(F32) == slot_column
            for first in range(0, slot_count, LANES)
        ],
        axis=1,
    ).astype(BF16)


def finish_kernel(
    feats_ref,
    pick_ref,
    returned_ref,
    w_out_ref,
    gain_ref,
    w_up_ref,
    w_down_ref,
    refined_ref,
):
    mixed = jnp.dot(pick_ref[...], returned_ref[...], preferred_element_type=F32).astype(BF16)
    resid = feats_ref[...].astype(F32) + jnp.dot(
        mixed, w_out_ref[...], preferred_element_type=F32
    )
    meansq = jnp.mean(resid * resid, axis=1, keepdims=True)
    normed = (resid * lax.rsqrt(meansq + 1e-05) * gain_ref[...]).astype(BF16)
    hidden = jax.nn.gelu(
        jnp.dot(normed, w_up_ref[...], preferred_element_type=F32), approximate=True
    ).astype(BF16)
    refined_ref[...] = (
        resid + jnp.dot(hidden, w_down_ref[...], preferred_element_type=F32)
    ).astype(BF16)


def params(mebibytes):
    return pltpu.CompilerParams(vmem_limit_bytes=mebibytes << 20)


def on_device(
    query_feats,
    query_region,
    neighbors,
    latents,
    w_query,
    w_key,
    w_value,
    w_out,
    norm_gain,
    w_up,
    w_down,
):
    region_count = lax.axis_size("region")
    shard_count = lax.axis_size("shard")
    chips = shard_count // 2
    query_count, width = query_feats.shape
    neighbor_count = neighbors.shape[1]
    capacity = min(query_count, 2 * query_count // region_count)
    slot_count = region_count * capacity
    table_rows = latents.shape[0] * chips
    region_row = query_region.reshape(1, query_count)
    payload = (region_count, width // LANES * capacity + capacity // 2, LANES)

    def fetch(table, even_step, odd_step):
        steps = (even_step, odd_step)
        pairs = [
            ((chip + steps[chip % 2]) % chips * 2 + core, chip * 2 + core)
            for chip in range(chips)
            for core in range(2)
        ]
        return lax.ppermute(table, "shard", pairs)

    def swap(table):
        return lax.ppermute(table, "shard", [(place, place ^ 1) for place in range(shard_count)])

    def join(pieces, flops, name):
        rows = sum(piece.shape[0] for piece in pieces)
        return pl.pallas_call(
            join_kernel,
            out_shape=jax.ShapeDtypeStruct((rows, width), BF16),
            in_specs=[VMEM] * len(pieces),
            out_specs=VMEM,
            compiler_params=params(4),
            cost_estimate=pl.CostEstimate(flops=flops, bytes_accessed=0, transcendentals=0),
            name=name,
        )(*pieces)

    def pack(early_turn, *begun):
        anywhere = pl.BlockSpec(memory_space=pl.ANY)
        return pl.pallas_call(
            functools.partial(pack_kernel, region_count, capacity, early_turn),
            out_shape=jax.ShapeDtypeStruct(payload, BF16),
            in_specs=[anywhere] * (4 + len(begun)),
            out_specs=anywhere,
            scratch_shapes=[
                pltpu.VMEM((query_count, width), BF16),
                pltpu.VMEM((1, query_count), jnp.int32),
                pltpu.VMEM((neighbor_count, query_count), jnp.int32),
                pltpu.VMEM((width, width), BF16),
                pltpu.VMEM(payload, BF16),
                pltpu.SemaphoreType.DMA((4,)),
                pltpu.SemaphoreType.DMA,
            ],
            input_output_aliases={4: 0} if begun else {},
            compiler_params=params(56),
            name="pack_early" if early_turn else "pack_late",
        )(query_feats, region_row, neighbors.T, w_query, *begun)

    begun, latents = lax.optimization_barrier((pack(True), latents))
    opposite = fetch(latents, 3, -3)
    send = pack(False, begun)
    received = lax.all_to_all(send, "region", split_axis=0, concat_axis=0, tiled=True)
    pair = join([latents, opposite], 10**11, "join_pair")
    pick = pl.pallas_call(
        functools.partial(pick_kernel, region_count, capacity),
        out_shape=jax.ShapeDtypeStruct((query_count, slot_count), BF16),
        in_specs=[VMEM] * 2,
        out_specs=VMEM,
        compiler_params=params(4),
        cost_estimate=pl.CostEstimate(flops=10**10, bytes_accessed=0, transcendentals=0),
        name="pick",
    )(region_row, pair)
    received, pick = lax.optimization_barrier((received, pick))
    logcount = pl.pallas_call(
        functools.partial(count_kernel, neighbor_count),
        out_shape=jax.ShapeDtypeStruct((chips, 2, latents.shape[0], slot_count), F32),
        in_specs=[VMEM],
        out_specs=VMEM,
        scratch_shapes=[
            pltpu.VMEM((slot_count // LANES, neighbor_count, LANES), jnp.int32),
            pltpu.VMEM((slot_count // LANES, neighbor_count, LANES), jnp.int32),
        ],
        compiler_params=params(8),
        name="count",
    )(received)
    arrivals = [fetch(pair, 1, 1), fetch(pair, -1, -1), fetch(pair, 2, -2)]
    arrivals, logcount = lax.optimization_barrier((arrivals, logcount))
    near = join([pair, *arrivals], 0, "join_near")
    far = swap(near)
    scratch = [
        pltpu.VMEM((table_rows, width), BF16),
        pltpu.VMEM((table_rows, width), BF16),
        pltpu.VMEM((width, table_rows), BF16),
    ]
    groups = slot_count // LANES * HEADS
    sums = pl.pallas_call(
        functools.partial(attend_kernel, True, latents.shape[0]),
        out_shape=[
            jax.ShapeDtypeStruct((groups, width // HEADS, LANES), F32),
            jax.ShapeDtypeStruct((groups, 8, LANES), F32),
        ],
        in_specs=[VMEM] * 5,
        out_specs=[VMEM] * 2,
        scratch_shapes=scratch,
        compiler_params=params(16),
        cost_estimate=pl.CostEstimate(flops=10**10, bytes_accessed=0, transcendentals=0),
        name="attend_near",
    )(received, logcount, near, w_key, w_value)
    mixed = pl.pallas_call(
        functools.partial(attend_kernel, False, latents.shape[0]),
        out_shape=jax.ShapeDtypeStruct((region_count, capacity, width), BF16),
        in_specs=[VMEM] * 7,
        out_specs=VMEM,
        scratch_shapes=scratch,
        compiler_params=params(16),
        name="attend_far",
    )(received, logcount, far, w_key, w_value, *sums)
    returned = lax.all_to_all(
        mixed, "region", split_axis=0, concat_axis=0, tiled=True
    ).reshape(slot_count, width)
    return pl.pallas_call(
        finish_kernel,
        out_shape=jax.ShapeDtypeStruct((query_count, width), BF16),
        in_specs=[VMEM] * 7,
        out_specs=VMEM,
        compiler_params=params(24),
        name="finish",
    )(query_feats, pick, returned, w_out, norm_gain.reshape(1, width), w_up, w_down)


def solution(mesh):
    in_specs = (P(("region", "shard"), None),) * 4 + (P(),) * 7
    out_specs = P(("region", "shard"), None)
    return jax.shard_map(
        on_device, mesh=mesh, in_specs=in_specs, out_specs=out_specs, check_vma=False
    )
```

```python
import functools
import math

import jax
import jax.numpy as jnp
from jax import lax
from jax.experimental import pallas as pl
from jax.experimental.pallas import tpu as pltpu
from jax.sharding import PartitionSpec as P

HEADS = 4
LANES = 128
ABSENT = -1e30
F32 = jnp.float32
BF16 = jnp.bfloat16
VMEM = pl.BlockSpec(memory_space=pltpu.VMEM)
NT = (((1,), (1,)), ((), ()))


def slots_of(region_row, region_count, capacity):
    rows = region_row.shape[1]
    onehot = (lax.broadcasted_iota(jnp.int32, (region_count, rows), 0) == region_row).astype(F32)
    earlier_than = lax.broadcasted_iota(jnp.int32, (rows, rows), 0) < lax.broadcasted_iota(
        jnp.int32, (rows, rows), 1
    )
    earlier = jnp.dot(onehot.astype(BF16), earlier_than.astype(BF16), preferred_element_type=F32)
    rank = jnp.sum(earlier * onehot, axis=0, keepdims=True)
    return region_row.astype(F32) * float(capacity) + rank


def pack_kernel(region_count, capacity, early_turn, *refs):
    feats_hbm, region_hbm, neighbors_hbm, w_query_hbm = refs[:4]
    send_hbm, feats_ref, region_ref, neighbors_ref, w_query_ref, send_ref, arrived, left = refs[-8:]
    early = lax.axis_index("shard") < lax.axis_size("shard") * 3 // 8

    @pl.when(early if early_turn else jnp.logical_not(early))
    def _():
        sources = (region_hbm, neighbors_hbm, feats_hbm, w_query_hbm)
        targets = (region_ref, neighbors_ref, feats_ref, w_query_ref)
        copies = [
            pltpu.make_async_copy(source, target, arrived.at[number])
            for number, (source, target) in enumerate(zip(sources, targets))
        ]
        for copy in copies:
            copy.start()
        slot_count = region_count * capacity
        rows, width = feats_ref.shape
        copies[0].wait()
        slot_row = slots_of(region_ref[...], region_count, capacity)
        place = (
            lax.broadcasted_iota(jnp.int32, (slot_count, rows), 0).astype(F32) == slot_row
        ).astype(BF16)
        copies[1].wait()
        number = neighbors_ref[...]
        coded = ((number & 127) + 128) << (number >> 7)
        coded = coded.astype(F32).astype(BF16)
        spread = lax.dot_general(place, coded, NT, preferred_element_type=F32)
        spread = spread.reshape(region_count, capacity, spread.shape[1])
        half = capacity // 2
        spread = jnp.concatenate([spread[:, :half], spread[:, half:]], axis=2)
        send_ref[:, width // LANES * capacity :, :] = spread.astype(BF16)
        copies[2].wait()
        copies[3].wait()
        query = jnp.dot(feats_ref[...], w_query_ref[...], preferred_element_type=F32)
        placed = jnp.dot(place, query.astype(BF16), preferred_element_type=F32).astype(BF16)
        for head in range(width // LANES):
            send_ref[:, head * capacity : (head + 1) * capacity, :] = placed[
                :, head * LANES : (head + 1) * LANES
            ].reshape(region_count, capacity, LANES)
        leaving = pltpu.make_async_copy(send_ref, send_hbm, left)
        leaving.start()
        leaving.wait()


def count_kernel(neighbor_count, received_ref, logcount_ref, low_ref, digit_ref):
    slot_count = logcount_ref.shape[3]
    sources, rows, _ = received_ref.shape
    half = slot_count // sources // 2
    coded = received_ref[:, rows - half :, :].astype(F32).reshape(sources * half, LANES)
    blocks = slot_count // LANES
    for pair in range(blocks // 2):
        both = jnp.transpose(coded[pair * LANES : (pair + 1) * LANES])
        for side in range(2):
            part = both[side * neighbor_count : (side + 1) * neighbor_count]
            high = jnp.zeros(part.shape, jnp.int32)
            for power in range(1, 8):
                high += (part >= float(128 << power)).astype(jnp.int32)
            number = (high - 1) * 128 + (part.astype(jnp.int32) >> high)
            low_ref[side * (blocks // 2) + pair] = number & 63
            digit_ref[side * (blocks // 2) + pair] = jnp.int32(1) << (2 * (number >> 6))

    size = 32

    def one(step, carry):
        block, base = step // 2, step % 2 * size
        lanes = pl.ds(pl.multiple_of(block * LANES, LANES), LANES)
        inside = pl.ds(pl.multiple_of(base, size), size)
        numbers = lax.broadcasted_iota(jnp.int32, (size, LANES), 0) + base
        wide = [0, 0, 0, 0]
        for first in range(0, neighbor_count, 15):
            last = min(first + 15, neighbor_count)
            middle = [0, 0]
            for start in range(first, last, 3):
                narrow = 0
                for k in range(start, min(start + 3, last)):
                    same = low_ref[block, k : k + 1, :] == numbers
                    narrow = narrow + jnp.where(same, digit_ref[block, k : k + 1, :], 0)
                middle[0] = middle[0] + (narrow & 0x33333333)
                middle[1] = middle[1] + ((narrow >> 2) & 0x33333333)
            for odd in range(2):
                wide[odd] = wide[odd] + (middle[odd] & 0x0F0F0F0F)
                wide[2 + odd] = wide[2 + odd] + ((middle[odd] >> 4) & 0x0F0F0F0F)
        for digit in range(16):
            count = (wide[digit % 4] >> (8 * (digit // 4))) & 0xFF
            logs = jnp.maximum(jnp.log2(count.astype(F32)), ABSENT)
            logcount_ref[digit // 2, digit % 2, inside, lanes] = logs
        return carry

    lax.fori_loop(0, blocks * 2, one, 0)


def join_kernel(*refs):
    joined_ref = refs[-1]
    first = 0
    for ref in refs[:-1]:
        rows = ref.shape[0]
        joined_ref[first : first + rows, :] = ref[...]
        first += rows


def attend_kernel(
    first_part,
    rows_held,
    received_ref,
    logcount_ref,
    table_ref,
    w_key_ref,
    w_value_ref,
    *refs,
):
    if first_part:
        mixed_out_ref, stats_out_ref, token_ref, key_ref, value_ref = refs
        sources, capacity = received_ref.shape[0], received_ref.shape[1] * 2 // (2 * HEADS + 1)
        width = w_key_ref.shape[1]
    else:
        mixed_in_ref, stats_in_ref, mixed_ref, token_ref, key_ref, value_ref = refs
        sources, capacity, width = mixed_ref.shape
    head_width = width // HEADS
    place = lax.axis_index("shard")
    chips = token_ref.shape[0] // rows_held
    chip, core = place // 2, place % 2
    if not first_part:
        core = 1 - core
    turn = 1 - 2 * (chip % 2)
    steps = (0, 3 * turn, -1, -1 - 3 * turn, 1, 1 - 3 * turn, 2 * turn, 5 * turn)
    for step, offset in enumerate(steps):
        origin = lax.rem(chip + offset + chips, chips)
        target = pl.ds(pl.multiple_of(origin * rows_held, rows_held), rows_held)
        token_ref[target, :] = table_ref[step * rows_held : (step + 1) * rows_held, :]
    tokens = token_ref[...]
    key_ref[...] = jnp.dot(tokens, w_key_ref[...], preferred_element_type=F32).astype(BF16)
    value_ref[...] = lax.dot_general(
        w_value_ref[...], tokens, (((0,), (1,)), ((), ())), preferred_element_type=F32
    ).astype(BF16)
    factor = head_width ** (-0.5) * math.log2(math.e)
    half, chunk = capacity // 2, 256
    group = LANES // half
    for block in range(sources * capacity // LANES):
        side, first_source = divmod(block * group, sources)
        senders = slice(first_source, first_source + group)
        lanes = slice(block * LANES, (block + 1) * LANES)
        for head in range(HEADS):
            columns = slice(head * head_width, (head + 1) * head_width)
            top = head * capacity + side * half
            query = received_ref[senders, top : top + half, :].reshape(LANES, head_width)
            number = block * HEADS + head
            if first_part:
                peak = jnp.full((1, LANES), 2 * ABSENT, F32)
                total = jnp.zeros((1, LANES), F32)
                mixed = jnp.zeros((head_width, LANES), F32)
            else:
                peak = stats_in_ref[number, 0:1, :]
                total = stats_in_ref[number, 1:2, :]
                mixed = mixed_in_ref[number]
            for first in range(0, key_ref.shape[0], chunk):
                part = slice(first, first + chunk)
                holders = slice(first // rows_held, (first + chunk) // rows_held)
                scores = lax.dot_general(
                    key_ref[part, columns], query, NT, preferred_element_type=F32
                )
                logcount = logcount_ref[holders, core, :, lanes].reshape(chunk, LANES)
                scores = scores * factor + logcount
                higher = jnp.maximum(peak, jnp.max(scores, axis=0, keepdims=True))
                raised = jnp.exp2(scores - higher)
                shrink = jnp.exp2(peak - higher)
                total = total * shrink + jnp.sum(raised, axis=0, keepdims=True)
                mixed = mixed * shrink + jnp.dot(
                    value_ref[columns, part], raised.astype(BF16), preferred_element_type=F32
                )
                peak = higher
            if first_part:
                mixed_out_ref[number] = mixed
                stats_out_ref[number, 0:1, :] = peak
                stats_out_ref[number, 1:2, :] = total
            else:
                mixed_ref[senders, side * half : (side + 1) * half, columns] = (
                    jnp.transpose(mixed / total).astype(BF16).reshape(group, half, head_width)
                )


def pick_kernel(region_count, capacity, region_ref, after_ref, pick_ref):
    rows, slot_count = pick_ref.shape
    slot_row = slots_of(region_ref[...], region_count, capacity)
    slot_column = jnp.transpose(jnp.broadcast_to(slot_row, (LANES, rows)))
    pick_ref[...] = jnp.concatenate(
        [
            (lax.broadcasted_iota(jnp.int32, (rows, LANES), 1) + first).astype(F32) == slot_column
            for first in range(0, slot_count, LANES)
        ],
        axis=1,
    ).astype(BF16)


def finish_kernel(
    feats_ref,
    pick_ref,
    returned_ref,
    w_out_ref,
    gain_ref,
    w_up_ref,
    w_down_ref,
    refined_ref,
):
    mixed = jnp.dot(pick_ref[...], returned_ref[...], preferred_element_type=F32).astype(BF16)
    resid = feats_ref[...].astype(F32) + jnp.dot(
        mixed, w_out_ref[...], preferred_element_type=F32
    )
    meansq = jnp.mean(resid * resid, axis=1, keepdims=True)
    normed = (resid * lax.rsqrt(meansq + 1e-05) * gain_ref[...]).astype(BF16)
    hidden = jax.nn.gelu(
        jnp.dot(normed, w_up_ref[...], preferred_element_type=F32), approximate=True
    ).astype(BF16)
    refined_ref[...] = (
        resid + jnp.dot(hidden, w_down_ref[...], preferred_element_type=F32)
    ).astype(BF16)


def params(mebibytes):
    return pltpu.CompilerParams(vmem_limit_bytes=mebibytes << 20)


def on_device(
    query_feats,
    query_region,
    neighbors,
    latents,
    w_query,
    w_key,
    w_value,
    w_out,
    norm_gain,
    w_up,
    w_down,
):
    region_count = lax.axis_size("region")
    shard_count = lax.axis_size("shard")
    chips = shard_count // 2
    query_count, width = query_feats.shape
    neighbor_count = neighbors.shape[1]
    capacity = min(query_count, 2 * query_count // region_count)
    slot_count = region_count * capacity
    table_rows = latents.shape[0] * chips
    region_row = query_region.reshape(1, query_count)
    payload = (region_count, width // LANES * capacity + capacity // 2, LANES)

    def fetch(table, even_step, odd_step):
        steps = (even_step, odd_step)
        pairs = [
            ((chip + steps[chip % 2]) % chips * 2 + core, chip * 2 + core)
            for chip in range(chips)
            for core in range(2)
        ]
        return lax.ppermute(table, "shard", pairs)

    def swap(table):
        return lax.ppermute(table, "shard", [(place, place ^ 1) for place in range(shard_count)])

    def join(pieces, flops, name):
        rows = sum(piece.shape[0] for piece in pieces)
        return pl.pallas_call(
            join_kernel,
            out_shape=jax.ShapeDtypeStruct((rows, width), BF16),
            in_specs=[VMEM] * len(pieces),
            out_specs=VMEM,
            compiler_params=params(4),
            cost_estimate=pl.CostEstimate(flops=flops, bytes_accessed=0, transcendentals=0),
            name=name,
        )(*pieces)

    def pack(early_turn, *begun):
        anywhere = pl.BlockSpec(memory_space=pl.ANY)
        return pl.pallas_call(
            functools.partial(pack_kernel, region_count, capacity, early_turn),
            out_shape=jax.ShapeDtypeStruct(payload, BF16),
            in_specs=[anywhere] * (4 + len(begun)),
            out_specs=anywhere,
            scratch_shapes=[
                pltpu.VMEM((query_count, width), BF16),
                pltpu.VMEM((1, query_count), jnp.int32),
                pltpu.VMEM((neighbor_count, query_count), jnp.int32),
                pltpu.VMEM((width, width), BF16),
                pltpu.VMEM(payload, BF16),
                pltpu.SemaphoreType.DMA((4,)),
                pltpu.SemaphoreType.DMA,
            ],
            input_output_aliases={4: 0} if begun else {},
            compiler_params=params(56),
            name="pack_early" if early_turn else "pack_late",
        )(query_feats, region_row, neighbors.T, w_query, *begun)

    begun, latents = lax.optimization_barrier((pack(True), latents))
    opposite = fetch(latents, 3, -3)
    send = pack(False, begun)
    received = lax.all_to_all(send, "region", split_axis=0, concat_axis=0, tiled=True)
    pair = join([latents, opposite], 10**11, "join_pair")
    pick = pl.pallas_call(
        functools.partial(pick_kernel, region_count, capacity),
        out_shape=jax.ShapeDtypeStruct((query_count, slot_count), BF16),
        in_specs=[VMEM] * 2,
        out_specs=VMEM,
        compiler_params=params(4),
        cost_estimate=pl.CostEstimate(flops=10**10, bytes_accessed=0, transcendentals=0),
        name="pick",
    )(region_row, pair)
    received, pick = lax.optimization_barrier((received, pick))
    logcount = pl.pallas_call(
        functools.partial(count_kernel, neighbor_count),
        out_shape=jax.ShapeDtypeStruct((chips, 2, latents.shape[0], slot_count), F32),
        in_specs=[VMEM],
        out_specs=VMEM,
        scratch_shapes=[
            pltpu.VMEM((slot_count // LANES, neighbor_count, LANES), jnp.int32),
            pltpu.VMEM((slot_count // LANES, neighbor_count, LANES), jnp.int32),
        ],
        compiler_params=params(8),
        name="count",
    )(received)
    arrivals = [fetch(pair, -1, -1), fetch(pair, 1, 1), fetch(pair, 2, -2)]
    arrivals, logcount = lax.optimization_barrier((arrivals, logcount))
    near = join([pair, *arrivals], 0, "join_near")
    far = swap(near)
    scratch = [
        pltpu.VMEM((table_rows, width), BF16),
        pltpu.VMEM((table_rows, width), BF16),
        pltpu.VMEM((width, table_rows), BF16),
    ]
    groups = slot_count // LANES * HEADS
    sums = pl.pallas_call(
        functools.partial(attend_kernel, True, latents.shape[0]),
        out_shape=[
            jax.ShapeDtypeStruct((groups, width // HEADS, LANES), F32),
            jax.ShapeDtypeStruct((groups, 8, LANES), F32),
        ],
        in_specs=[VMEM] * 5,
        out_specs=[VMEM] * 2,
        scratch_shapes=scratch,
        compiler_params=params(16),
        cost_estimate=pl.CostEstimate(flops=10**10, bytes_accessed=0, transcendentals=0),
        name="attend_near",
    )(received, logcount, near, w_key, w_value)
    mixed = pl.pallas_call(
        functools.partial(attend_kernel, False, latents.shape[0]),
        out_shape=jax.ShapeDtypeStruct((region_count, capacity, width), BF16),
        in_specs=[VMEM] * 7,
        out_specs=VMEM,
        scratch_shapes=scratch,
        compiler_params=params(16),
        name="attend_far",
    )(received, logcount, far, w_key, w_value, *sums)
    returned = lax.all_to_all(
        mixed, "region", split_axis=0, concat_axis=0, tiled=True
    ).reshape(slot_count, width)
    return pl.pallas_call(
        finish_kernel,
        out_shape=jax.ShapeDtypeStruct((query_count, width), BF16),
        in_specs=[VMEM] * 7,
        out_specs=VMEM,
        compiler_params=params(24),
        name="finish",
    )(query_feats, pick, returned, w_out, norm_gain.reshape(1, width), w_up, w_down)


def solution(mesh):
    in_specs = (P(("region", "shard"), None),) * 4 + (P(),) * 7
    out_specs = P(("region", "shard"), None)
    return jax.shard_map(
        on_device, mesh=mesh, in_specs=in_specs, out_specs=out_specs, check_vma=False
    )
```

```python
import functools
import math

import jax
import jax.numpy as jnp
from jax import lax
from jax.experimental import pallas as pl
from jax.experimental.pallas import tpu as pltpu
from jax.sharding import PartitionSpec as P

HEADS = 4
LANES = 128
ABSENT = -1e30
F32 = jnp.float32
BF16 = jnp.bfloat16
VMEM = pl.BlockSpec(memory_space=pltpu.VMEM)
NT = (((1,), (1,)), ((), ()))


def slots_of(region_row, region_count, capacity):
    rows = region_row.shape[1]
    onehot = (lax.broadcasted_iota(jnp.int32, (region_count, rows), 0) == region_row).astype(F32)
    earlier_than = lax.broadcasted_iota(jnp.int32, (rows, rows), 0) < lax.broadcasted_iota(
        jnp.int32, (rows, rows), 1
    )
    earlier = jnp.dot(onehot.astype(BF16), earlier_than.astype(BF16), preferred_element_type=F32)
    rank = jnp.sum(earlier * onehot, axis=0, keepdims=True)
    return region_row.astype(F32) * float(capacity) + rank


def pack_kernel(region_count, capacity, early_turn, *refs):
    feats_hbm, region_hbm, neighbors_hbm, w_query_hbm = refs[:4]
    send_hbm, feats_ref, region_ref, neighbors_ref, w_query_ref, send_ref, arrived, left = refs[-8:]
    early = lax.axis_index("shard") < lax.axis_size("shard") * 3 // 8

    @pl.when(early if early_turn else jnp.logical_not(early))
    def _():
        sources = (region_hbm, neighbors_hbm, feats_hbm, w_query_hbm)
        targets = (region_ref, neighbors_ref, feats_ref, w_query_ref)
        copies = [
            pltpu.make_async_copy(source, target, arrived.at[number])
            for number, (source, target) in enumerate(zip(sources, targets))
        ]
        for copy in reversed(copies):
            copy.start()
        slot_count = region_count * capacity
        rows, width = feats_ref.shape
        copies[0].wait()
        slot_row = slots_of(region_ref[...], region_count, capacity)
        place = (
            lax.broadcasted_iota(jnp.int32, (slot_count, rows), 0).astype(F32) == slot_row
        ).astype(BF16)
        copies[1].wait()
        number = neighbors_ref[...]
        coded = ((number & 127) + 128) << (number >> 7)
        coded = coded.astype(F32).astype(BF16)
        spread = lax.dot_general(place, coded, NT, preferred_element_type=F32)
        spread = spread.reshape(region_count, capacity, spread.shape[1])
        half = capacity // 2
        spread = jnp.concatenate([spread[:, :half], spread[:, half:]], axis=2)
        send_ref[:, width // LANES * capacity :, :] = spread.astype(BF16)
        copies[2].wait()
        copies[3].wait()
        query = jnp.dot(feats_ref[...], w_query_ref[...], preferred_element_type=F32)
        placed = jnp.dot(place, query.astype(BF16), preferred_element_type=F32).astype(BF16)
        for head in range(width // LANES):
            send_ref[:, head * capacity : (head + 1) * capacity, :] = placed[
                :, head * LANES : (head + 1) * LANES
            ].reshape(region_count, capacity, LANES)
        leaving = pltpu.make_async_copy(send_ref, send_hbm, left)
        leaving.start()
        leaving.wait()


def count_kernel(neighbor_count, received_ref, logcount_ref, low_ref, digit_ref):
    slot_count = logcount_ref.shape[3]
    sources, rows, _ = received_ref.shape
    half = slot_count // sources // 2
    coded = received_ref[:, rows - half :, :].astype(F32).reshape(sources * half, LANES)
    blocks = slot_count // LANES
    for pair in range(blocks // 2):
        both = jnp.transpose(coded[pair * LANES : (pair + 1) * LANES])
        for side in range(2):
            part = both[side * neighbor_count : (side + 1) * neighbor_count]
            high = jnp.zeros(part.shape, jnp.int32)
            for power in range(1, 8):
                high += (part >= float(128 << power)).astype(jnp.int32)
            number = (high - 1) * 128 + (part.astype(jnp.int32) >> high)
            low_ref[side * (blocks // 2) + pair] = number & 63
            digit_ref[side * (blocks // 2) + pair] = jnp.int32(1) << (2 * (number >> 6))

    size = 32

    def one(step, carry):
        block, base = step // 2, step % 2 * size
        lanes = pl.ds(pl.multiple_of(block * LANES, LANES), LANES)
        inside = pl.ds(pl.multiple_of(base, size), size)
        numbers = lax.broadcasted_iota(jnp.int32, (size, LANES), 0) + base
        wide = [0, 0, 0, 0]
        for first in range(0, neighbor_count, 15):
            last = min(first + 15, neighbor_count)
            middle = [0, 0]
            for start in range(first, last, 3):
                narrow = 0
                for k in range(start, min(start + 3, last)):
                    same = low_ref[block, k : k + 1, :] == numbers
                    narrow = narrow + jnp.where(same, digit_ref[block, k : k + 1, :], 0)
                middle[0] = middle[0] + (narrow & 0x33333333)
                middle[1] = middle[1] + ((narrow >> 2) & 0x33333333)
            for odd in range(2):
                wide[odd] = wide[odd] + (middle[odd] & 0x0F0F0F0F)
                wide[2 + odd] = wide[2 + odd] + ((middle[odd] >> 4) & 0x0F0F0F0F)
        for digit in range(16):
            count = (wide[digit % 4] >> (8 * (digit // 4))) & 0xFF
            logs = jnp.maximum(jnp.log2(count.astype(F32)), ABSENT)
            logcount_ref[digit // 2, digit % 2, inside, lanes] = logs
        return carry

    lax.fori_loop(0, blocks * 2, one, 0)


def join_kernel(*refs):
    joined_ref = refs[-1]
    first = 0
    for ref in refs[:-1]:
        rows = ref.shape[0]
        joined_ref[first : first + rows, :] = ref[...]
        first += rows


def attend_kernel(
    first_part,
    rows_held,
    received_ref,
    logcount_ref,
    table_ref,
    w_key_ref,
    w_value_ref,
    *refs,
):
    if first_part:
        mixed_out_ref, stats_out_ref, token_ref, key_ref, value_ref = refs
        sources, capacity = received_ref.shape[0], received_ref.shape[1] * 2 // (2 * HEADS + 1)
        width = w_key_ref.shape[1]
    else:
        mixed_in_ref, stats_in_ref, mixed_ref, token_ref, key_ref, value_ref = refs
        sources, capacity, width = mixed_ref.shape
    head_width = width // HEADS
    place = lax.axis_index("shard")
    chips = token_ref.shape[0] // rows_held
    chip, core = place // 2, place % 2
    if not first_part:
        core = 1 - core
    turn = 1 - 2 * (chip % 2)
    steps = (0, 3 * turn, 1, 1 - 3 * turn, -1, -1 - 3 * turn, 2 * turn, 5 * turn)
    for step, offset in enumerate(steps):
        origin = lax.rem(chip + offset + chips, chips)
        target = pl.ds(pl.multiple_of(origin * rows_held, rows_held), rows_held)
        token_ref[target, :] = table_ref[step * rows_held : (step + 1) * rows_held, :]
    tokens = token_ref[...]
    key_ref[...] = jnp.dot(tokens, w_key_ref[...], preferred_element_type=F32).astype(BF16)
    value_ref[...] = lax.dot_general(
        w_value_ref[...], tokens, (((0,), (1,)), ((), ())), preferred_element_type=F32
    ).astype(BF16)
    factor = head_width ** (-0.5) * math.log2(math.e)
    half, chunk = capacity // 2, 256
    group = LANES // half
    for block in range(sources * capacity // LANES):
        side, first_source = divmod(block * group, sources)
        senders = slice(first_source, first_source + group)
        lanes = slice(block * LANES, (block + 1) * LANES)
        for head in range(HEADS):
            columns = slice(head * head_width, (head + 1) * head_width)
            top = head * capacity + side * half
            query = received_ref[senders, top : top + half, :].reshape(LANES, head_width)
            number = block * HEADS + head
            if first_part:
                peak = jnp.full((1, LANES), 2 * ABSENT, F32)
                total = jnp.zeros((1, LANES), F32)
                mixed = jnp.zeros((head_width, LANES), F32)
            else:
                peak = stats_in_ref[number, 0:1, :]
                total = stats_in_ref[number, 1:2, :]
                mixed = mixed_in_ref[number]
            for first in range(0, key_ref.shape[0], chunk):
                part = slice(first, first + chunk)
                holders = slice(first // rows_held, (first + chunk) // rows_held)
                scores = lax.dot_general(
                    key_ref[part, columns], query, NT, preferred_element_type=F32
                )
                logcount = logcount_ref[holders, core, :, lanes].reshape(chunk, LANES)
                scores = scores * factor + logcount
                higher = jnp.maximum(peak, jnp.max(scores, axis=0, keepdims=True))
                raised = jnp.exp2(scores - higher)
                shrink = jnp.exp2(peak - higher)
                total = total * shrink + jnp.sum(raised, axis=0, keepdims=True)
                mixed = mixed * shrink + jnp.dot(
                    value_ref[columns, part], raised.astype(BF16), preferred_element_type=F32
                )
                peak = higher
            if first_part:
                mixed_out_ref[number] = mixed
                stats_out_ref[number, 0:1, :] = peak
                stats_out_ref[number, 1:2, :] = total
            else:
                mixed_ref[senders, side * half : (side + 1) * half, columns] = (
                    jnp.transpose(mixed / total).astype(BF16).reshape(group, half, head_width)
                )


def pick_kernel(region_count, capacity, region_ref, after_ref, pick_ref):
    rows, slot_count = pick_ref.shape
    slot_row = slots_of(region_ref[...], region_count, capacity)
    slot_column = jnp.transpose(jnp.broadcast_to(slot_row, (LANES, rows)))
    pick_ref[...] = jnp.concatenate(
        [
            (lax.broadcasted_iota(jnp.int32, (rows, LANES), 1) + first).astype(F32) == slot_column
            for first in range(0, slot_count, LANES)
        ],
        axis=1,
    ).astype(BF16)


def finish_kernel(
    feats_ref,
    pick_ref,
    returned_ref,
    w_out_ref,
    gain_ref,
    w_up_ref,
    w_down_ref,
    refined_ref,
):
    mixed = jnp.dot(pick_ref[...], returned_ref[...], preferred_element_type=F32).astype(BF16)
    resid = feats_ref[...].astype(F32) + jnp.dot(
        mixed, w_out_ref[...], preferred_element_type=F32
    )
    meansq = jnp.mean(resid * resid, axis=1, keepdims=True)
    normed = (resid * lax.rsqrt(meansq + 1e-05) * gain_ref[...]).astype(BF16)
    hidden = jax.nn.gelu(
        jnp.dot(normed, w_up_ref[...], preferred_element_type=F32), approximate=True
    ).astype(BF16)
    refined_ref[...] = (
        resid + jnp.dot(hidden, w_down_ref[...], preferred_element_type=F32)
    ).astype(BF16)


def params(mebibytes):
    return pltpu.CompilerParams(vmem_limit_bytes=mebibytes << 20)


def on_device(
    query_feats,
    query_region,
    neighbors,
    latents,
    w_query,
    w_key,
    w_value,
    w_out,
    norm_gain,
    w_up,
    w_down,
):
    region_count = lax.axis_size("region")
    shard_count = lax.axis_size("shard")
    chips = shard_count // 2
    query_count, width = query_feats.shape
    neighbor_count = neighbors.shape[1]
    capacity = min(query_count, 2 * query_count // region_count)
    slot_count = region_count * capacity
    table_rows = latents.shape[0] * chips
    region_row = query_region.reshape(1, query_count)
    payload = (region_count, width // LANES * capacity + capacity // 2, LANES)

    def fetch(table, even_step, odd_step):
        steps = (even_step, odd_step)
        pairs = [
            ((chip + steps[chip % 2]) % chips * 2 + core, chip * 2 + core)
            for chip in range(chips)
            for core in range(2)
        ]
        return lax.ppermute(table, "shard", pairs)

    def swap(table):
        return lax.ppermute(table, "shard", [(place, place ^ 1) for place in range(shard_count)])

    def join(pieces, flops, name):
        rows = sum(piece.shape[0] for piece in pieces)
        return pl.pallas_call(
            join_kernel,
            out_shape=jax.ShapeDtypeStruct((rows, width), BF16),
            in_specs=[VMEM] * len(pieces),
            out_specs=VMEM,
            compiler_params=params(4),
            cost_estimate=pl.CostEstimate(flops=flops, bytes_accessed=0, transcendentals=0),
            name=name,
        )(*pieces)

    def pack(early_turn, *begun):
        anywhere = pl.BlockSpec(memory_space=pl.ANY)
        return pl.pallas_call(
            functools.partial(pack_kernel, region_count, capacity, early_turn),
            out_shape=jax.ShapeDtypeStruct(payload, BF16),
            in_specs=[anywhere] * (4 + len(begun)),
            out_specs=anywhere,
            scratch_shapes=[
                pltpu.VMEM((query_count, width), BF16),
                pltpu.VMEM((1, query_count), jnp.int32),
                pltpu.VMEM((neighbor_count, query_count), jnp.int32),
                pltpu.VMEM((width, width), BF16),
                pltpu.VMEM(payload, BF16),
                pltpu.SemaphoreType.DMA((4,)),
                pltpu.SemaphoreType.DMA,
            ],
            input_output_aliases={4: 0} if begun else {},
            compiler_params=params(56),
            name="pack_early" if early_turn else "pack_late",
        )(query_feats, region_row, neighbors.T, w_query, *begun)

    begun, latents = lax.optimization_barrier((pack(True), latents))
    opposite = fetch(latents, 3, -3)
    send = pack(False, begun)
    received = lax.all_to_all(send, "region", split_axis=0, concat_axis=0, tiled=True)
    pair = join([latents, opposite], 10**11, "join_pair")
    pick = pl.pallas_call(
        functools.partial(pick_kernel, region_count, capacity),
        out_shape=jax.ShapeDtypeStruct((query_count, slot_count), BF16),
        in_specs=[VMEM] * 2,
        out_specs=VMEM,
        compiler_params=params(4),
        cost_estimate=pl.CostEstimate(flops=10**10, bytes_accessed=0, transcendentals=0),
        name="pick",
    )(region_row, pair)
    received, pick = lax.optimization_barrier((received, pick))
    logcount = pl.pallas_call(
        functools.partial(count_kernel, neighbor_count),
        out_shape=jax.ShapeDtypeStruct((chips, 2, latents.shape[0], slot_count), F32),
        in_specs=[VMEM],
        out_specs=VMEM,
        scratch_shapes=[
            pltpu.VMEM((slot_count // LANES, neighbor_count, LANES), jnp.int32),
            pltpu.VMEM((slot_count // LANES, neighbor_count, LANES), jnp.int32),
        ],
        compiler_params=params(8),
        name="count",
    )(received)
    arrivals = [fetch(pair, 1, 1), fetch(pair, -1, -1), fetch(pair, 2, -2)]
    arrivals, logcount = lax.optimization_barrier((arrivals, logcount))
    near = join([pair, *arrivals], 0, "join_near")
    far = swap(near)
    scratch = [
        pltpu.VMEM((table_rows, width), BF16),
        pltpu.VMEM((table_rows, width), BF16),
        pltpu.VMEM((width, table_rows), BF16),
    ]
    groups = slot_count // LANES * HEADS
    sums = pl.pallas_call(
        functools.partial(attend_kernel, True, latents.shape[0]),
        out_shape=[
            jax.ShapeDtypeStruct((groups, width // HEADS, LANES), F32),
            jax.ShapeDtypeStruct((groups, 8, LANES), F32),
        ],
        in_specs=[VMEM] * 5,
        out_specs=[VMEM] * 2,
        scratch_shapes=scratch,
        compiler_params=params(16),
        cost_estimate=pl.CostEstimate(flops=10**10, bytes_accessed=0, transcendentals=0),
        name="attend_near",
    )(received, logcount, near, w_key, w_value)
    mixed = pl.pallas_call(
        functools.partial(attend_kernel, False, latents.shape[0]),
        out_shape=jax.ShapeDtypeStruct((region_count, capacity, width), BF16),
        in_specs=[VMEM] * 7,
        out_specs=VMEM,
        scratch_shapes=scratch,
        compiler_params=params(16),
        name="attend_far",
    )(received, logcount, far, w_key, w_value, *sums)
    returned = lax.all_to_all(
        mixed, "region", split_axis=0, concat_axis=0, tiled=True
    ).reshape(slot_count, width)
    return pl.pallas_call(
        finish_kernel,
        out_shape=jax.ShapeDtypeStruct((query_count, width), BF16),
        in_specs=[VMEM] * 7,
        out_specs=VMEM,
        compiler_params=params(24),
        name="finish",
    )(query_feats, pick, returned, w_out, norm_gain.reshape(1, width), w_up, w_down)


def solution(mesh):
    in_specs = (P(("region", "shard"), None),) * 4 + (P(),) * 7
    out_specs = P(("region", "shard"), None)
    return jax.shard_map(
        on_device, mesh=mesh, in_specs=in_specs, out_specs=out_specs, check_vma=False
    )
```
